512 devices in a mesh: role: 2 (over x_lo), grp: 16 (over z), tp: 16 (over y, x_hi, core).
Axes of the slice: x: 4 (x_hi: 2, x_lo: 2; x = x_hi * 2 + x_lo), y: 4, z: 16, core: 2. Of those that a mesh axis runs over, the one named last changes fastest.
Arguments:
- prompt_acts: bfloat16 [2, 16, 1024, 8192], P('role', 'grp', None, 'tp'), may hold values from -6 to 6
- kv_weight: bfloat16 [8192, 2048], P('tp'), may hold values from -0.0625 to 0.0625
- cache_kv: bfloat16 [2, 32, 3072, 2048], P('role', 'grp', 'tp'), may hold values from -6 to 6
- cache_len: int32 [2, 32], P('role', 'grp'), may hold values from 1 to 3072, as said below
- block_owner: int32 [2, 32, 16], P('role', 'grp'), may hold values from 0 to 15, each once within a row
- span_row: int32 [2, 16], P('role', 'grp'), may hold values from 0 to 1
- draft_query: bfloat16 [2, 32, 4, 8192], P('role', 'grp')
- draft_kv: bfloat16 [2, 32, 4, 2048], P('role', 'grp'), may hold values from -4 to 4
Outputs:
- attn_out: bfloat16 [2, 32, 4, 8192], P('role', 'grp')
The draws below stay inside these ranges and needn't reach their ends.
Inputs may be any that keep to these rules, and one draw needn't show every extreme that they name: `cache_len`: some row of each pool has 3072 live positions. `block_owner`: each row's entries are a permutation of the slabs.
All inputs are finite; a program needn't handle non-finite values.
Results may differ from the reference program's by a relative error of at most 0.02.
Values may be sent and summed in bfloat16 or wider, within the bound.
No kernel may reach another device: no remote copies, remote signals or barrier semaphores. Data moves between devices by JAX's collectives and lax.ppermute only.
A program may use at most 64 MiB of HBM per device.

```python
import math
import jax
import jax.numpy as jnp
from jax import lax

D = 8192
QH = 64
KVH = 8
HD = 128
KVW = 2048
SPAN = 1024
ROWS_GRP = 2
ROWS = 32
L_DEV = 192
CACHE = 3072
DRAFT = 4
N_ROLE = 2
N_GRP = 16
N_TP = 16


def draft_noise(key):
    first = jax.random.fold_in(key, 0)
    shape = (2, ROWS, DRAFT, 2 * KVH * HD)
    gauss = jnp.clip(jax.random.normal(first, shape, jnp.float32), -4.0, 4.0)
    return gauss


def draw_draft_kv(key, part):
    gauss = draft_noise(key)
    values = gauss
    return values.astype(jnp.bfloat16)


def draw_draft_query(key, part):
    key = jax.random.fold_in(key, 5)
    first = jax.random.fold_in(key, 0)
    shape = (2, ROWS, DRAFT, QH * HD)
    values = jnp.clip(2.0 * jax.random.normal(first, shape, jnp.float32), -8.0, 8.0)
    return values.astype(jnp.bfloat16)


def draw_cache_len(key, part):
    key = jax.random.fold_in(key, 3)
    first, second = jax.random.split(key)
    lens = jax.random.randint(first, (2, ROWS), 1, CACHE + 1, dtype=jnp.int32)
    longest = jax.random.randint(second, (2, 1), 0, ROWS, dtype=jnp.int32)
    return jnp.where(jnp.arange(ROWS, dtype=jnp.int32)[None, :] == longest, CACHE, lens).astype(jnp.int32)


def set_ends(array, key, low, top_value):
    longest = array.shape.index(max(array.shape))
    spots = []
    for shift in (0, 1):
        where = [jax.random.randint(jax.random.fold_in(key, axis), (), 0, length) for axis, length in enumerate(array.shape)]
        where[longest] = (where[longest] + shift) % array.shape[longest]
        spots.append(tuple(where))
    return array.at[spots[0]].set(low).at[spots[1]].set(top_value)


def block_levels(key, extent, shards, low, largest):
    loudness = 1.0
    for axis_at, parts in shards:
        draws = jax.random.uniform(jax.random.fold_in(jax.random.fold_in(key, 6), axis_at), (parts,), jnp.float32, low / len(shards), largest / len(shards))
        loudness = loudness * jnp.repeat(jnp.exp(draws), extent[axis_at] // parts).reshape((-1,) + (1,) * (len(extent) - 1 - axis_at))
    return loudness


def scatter_about(own_key, extent, deviation, bound, cuts=(), held_as=jnp.bfloat16):
    result = jax.random.normal(own_key, extent, jnp.float32) * deviation
    if len(cuts) > 0:
        result = block_levels(own_key, extent, cuts, -0.22, 0.18) * result
    return jnp.clip(result, min=-bound, max=bound).astype(held_as)


def setup_inputs(seed: int = 0) -> dict:
    key_of = jax.random.split(jax.random.key(seed), 9)
    prompt_acts = scatter_about(key_of[0], (N_ROLE, N_GRP, SPAN, D), 1.0, 6.0, ((0, 2), (1, 16), (3, 16)))
    kv_weight = scatter_about(key_of[1], (D, KVW), D ** -0.5, 0.0625, ((0, 16),))
    cache_kv = scatter_about(key_of[2], (N_ROLE, ROWS, CACHE, KVW), 1.0, 6.0, ((0, 2), (1, 16), (2, 16)))
    cache_len = draw_cache_len(jax.random.fold_in(key_of[8], 71), 0)
    block_owner = jax.vmap(lambda own: jax.random.permutation(own, N_TP))(jax.random.split(key_of[4], N_ROLE * ROWS)).reshape((N_ROLE, ROWS, N_TP)).astype(jnp.int32)
    span_row = set_ends(jax.random.randint(key_of[5], (N_ROLE, N_GRP), 0, ROWS_GRP), jax.random.fold_in(key_of[5], 1), 0, ROWS_GRP - 1).astype(jnp.int32)
    draft_query = draw_draft_query(jax.random.fold_in(key_of[8], 71), 0)
    draft_kv = draw_draft_kv(jax.random.fold_in(key_of[8], 71), 0)
    return dict(prompt_acts=prompt_acts, kv_weight=kv_weight, cache_kv=cache_kv, cache_len=cache_len, block_owner=block_owner, span_row=span_row, draft_query=draft_query, draft_kv=draft_kv)


NEG = -1e+30

def reference(prompt_acts, kv_weight, cache_kv, cache_len, block_owner, span_row, draft_query, draft_kv):
    width = D // N_TP
    head_cols = KVH * HD
    qgroup = QH // KVH
    blocks = jnp.arange(N_TP, dtype=jnp.int32)
    scale = 1.0 / math.sqrt(HD)

    def project(acts):

        def step(total, block):
            left = lax.dynamic_slice_in_dim(acts, block * width, width, 1)
            right = lax.dynamic_slice_in_dim(kv_weight, block * width, width, 0)
            part = jnp.dot(left, right, preferred_element_type=jnp.float32).astype(jnp.bfloat16)
            part = lax.optimization_barrier(part)
            return (total + part.astype(jnp.float32), None)
        total, _ = lax.scan(step, jnp.zeros((SPAN, 2 * head_cols), jnp.float32), blocks)
        return total.astype(jnp.bfloat16)
    fresh = lax.map(project, prompt_acts.reshape(2 * N_GRP, SPAN, D))
    fresh = fresh.reshape(2, N_GRP, SPAN, 2 * head_cols)
    causal = jnp.arange(DRAFT)[:, None] >= jnp.arange(DRAFT)[None, :]
    results = []
    for pool in range(2):
        source = fresh[1 - pool]

        def one_row(row):
            grp_index = row // ROWS_GRP
            slot = row % ROWS_GRP
            owners = block_owner[pool][row]
            first = lax.optimization_barrier(jnp.sum(blocks[None, :] * (owners[None, :] == blocks[:, None]).astype(jnp.int32), axis=1))
            position = (first[:, None] * L_DEV + jnp.arange(L_DEV, dtype=jnp.int32)[None, :]).reshape(CACHE)
            live = position < cache_len[pool][row]
            taken = jnp.broadcast_to(span_row[pool][grp_index] == slot, (SPAN,))
            keys = jnp.concatenate([cache_kv[pool][row], source[grp_index], draft_kv[pool][row]], axis=0).astype(jnp.float32)
            mask = jnp.concatenate([jnp.broadcast_to(live[None, :], (DRAFT, CACHE)), jnp.broadcast_to(taken[None, :], (DRAFT, SPAN)), causal], axis=1)
            query = draft_query[pool][row].astype(jnp.float32).reshape(DRAFT, KVH, qgroup, HD)
            key_part = keys[:, :head_cols].reshape(-1, KVH, HD)
            value_part = keys[:, head_cols:].reshape(-1, KVH, HD)
            score = jnp.einsum('tkgd,lkd->kgtl', query, key_part) * scale
            score = jnp.where(mask[None, None], score, NEG)
            top = lax.optimization_barrier(jnp.max(score, axis=-1, keepdims=True))
            weight = jnp.where(mask[None, None], jnp.exp(score - top), 0.0)
            total = lax.optimization_barrier(jnp.sum(weight, axis=-1))
            rounded = lax.optimization_barrier(weight.astype(jnp.bfloat16)).astype(jnp.float32)
            summed = jnp.einsum('kgtl,lkd->kgtd', rounded, value_part)
            output = summed / total[..., None]
            return output.transpose(2, 0, 1, 3).reshape(DRAFT, QH * HD).astype(jnp.bfloat16)
        results.append(lax.map(one_row, jnp.arange(ROWS, dtype=jnp.int32)))
    return jnp.stack(results)
```

```python
import functools
import math

import jax
import jax.numpy as jnp
from jax import lax
from jax.experimental import pallas as pl
from jax.experimental.pallas import tpu as pltpu
from jax.sharding import Mesh
from jax.sharding import PartitionSpec as P

QH = 64
KVH = 8
HD = 128
DRAFT = 4
GROUP = QH // KVH
QROWS = GROUP * DRAFT
COLS = KVH * HD
NEG = -1e30
SCALE = 1.0 / math.sqrt(HD)

f32 = jnp.float32
bf16 = jnp.bfloat16


def dot_nt(a, b):
    return lax.dot_general(a, b, (((1,), (1,)), ((), ())), preferred_element_type=f32)


def dot_nn(a, b):
    return jnp.dot(a, b, preferred_element_type=f32)


def packed_stat(lse):
    hi = lse.astype(bf16).astype(f32)
    mid = (lse - hi).astype(bf16).astype(f32)
    lo = lse - hi - mid
    lane = lax.broadcasted_iota(jnp.int32, (lse.shape[0], HD), 1)
    return jnp.where(
        lane == 0, hi, jnp.where(lane == 1, mid, jnp.where(lane == 2, lo, 0.0))
    ).astype(bf16)


def stat(tile):
    return jnp.sum(tile.astype(f32), axis=-1, keepdims=True)


def attend(score, value):
    top = jnp.max(score, axis=-1, keepdims=True)
    weight = jnp.where(score > 0.5 * NEG, jnp.exp(score - top), 0.0)
    total = jnp.sum(weight, axis=-1, keepdims=True)
    any_key = total > 0.0
    safe = jnp.where(any_key, total, 1.0)
    out = dot_nn(weight.astype(bf16), value) / safe
    return out, jnp.where(any_key, top + jnp.log(safe), NEG)


def merge(parts):
    top = functools.reduce(jnp.maximum, [lse for _, lse in parts])
    weights = [jnp.where(lse > 0.5 * NEG, jnp.exp(lse - top), 0.0) for _, lse in parts]
    total = functools.reduce(jnp.add, weights)
    safe = jnp.where(total > 0.0, total, 1.0)
    out = functools.reduce(jnp.add, [w * o for w, (o, _) in zip(weights, parts)])
    return out / safe, jnp.where(total > 0.0, top + jnp.log(safe), NEG)


def cache_kernel(owner_ref, len_ref, q_ref, cache_ref, mine_ref, other_ref):
    core = lax.axis_index("core")
    me = lax.axis_index("yx") * 2 + core
    slab = cache_ref.shape[1]
    for which, out_ref in ((0, other_ref), (1, mine_ref)):
        row = core if which == 1 else 1 - core
        first = jnp.int32(0)
        for block in range(owner_ref.shape[1]):
            first = first + jnp.where(owner_ref[row, block] == me, block, 0)
        room = len_ref[0, row] - first * slab
        live = lax.broadcasted_iota(jnp.int32, (QROWS, slab), 1) < room
        for head in range(KVH):
            keys = cache_ref[row, :, head * HD : (head + 1) * HD]
            values = cache_ref[row, :, COLS + head * HD : COLS + (head + 1) * HD]
            score = dot_nt(q_ref[row, head], keys) * SCALE
            out, lse = attend(jnp.where(live, score, NEG), values)
            out_ref[head, :QROWS] = out.astype(bf16)
            out_ref[head, QROWS:] = packed_stat(lse)


def project_kernel(
    acts_ref, acts2_ref, w_ref, w2_ref, q_ref, mine_ref, theirs_ref, out_ref, qw_ref
):
    core = lax.axis_index("core")
    half = acts2_ref.shape[0]
    acts = acts_ref[pl.ds(pl.multiple_of(core * half, half), half), :]
    acts2 = acts2_ref[...]
    for head in range(KVH):
        cols = slice(head * HD, (head + 1) * HD)
        rows = slice(head * QROWS, (head + 1) * QROWS)
        qw_ref[0, rows] = dot_nt(q_ref[head], w_ref[:, cols]).astype(bf16)
        qw_ref[1, rows] = dot_nt(q_ref[head], w2_ref[:, cols]).astype(bf16)
    score = (dot_nt(qw_ref[0], acts) + dot_nt(qw_ref[1], acts2)) * SCALE
    high = score.astype(bf16)
    low = (score - high.astype(f32)).astype(bf16)
    tiles = half // HD
    for head in range(KVH):
        rows = slice(head * QROWS, (head + 1) * QROWS)
        for tile in range(tiles):
            cols = slice(tile * HD, (tile + 1) * HD)
            at = half + tile * QROWS
            out_ref[head, at : at + QROWS] = high[rows, cols]
            at = half + (tiles + tile) * QROWS
            out_ref[head, at : at + QROWS] = low[rows, cols]
        cols = slice(COLS + head * HD, COLS + (head + 1) * HD)
        value = dot_nn(acts, w_ref[:, cols]) + dot_nn(acts2, w2_ref[:, cols])
        out_ref[head, :half] = value.astype(bf16)
        out, lse = merge(
            [
                (ref[head, :QROWS].astype(f32), stat(ref[head, QROWS:]))
                for ref in (mine_ref, theirs_ref)
            ]
        )
        at = half + 2 * tiles * QROWS
        out_ref[head, at : at + QROWS] = out.astype(bf16)
        out_ref[head, at + QROWS : at + 2 * QROWS] = packed_stat(lse)


def span_kernel(got_ref, q_ref, draft_ref, out_ref):
    parts, length, _ = got_ref.shape
    half = (length - 2 * QROWS) * HD // (HD + 2 * QROWS)
    tiles = half // HD
    role = lax.axis_index("role")
    core = lax.axis_index("core")
    head = lax.axis_index("yx")

    def total(start, size):
        acc = got_ref[0, start : start + size].astype(f32)
        for part in range(1, parts):
            acc = acc + got_ref[part, start : start + size].astype(f32)
        return acc

    value = total(0, half).astype(bf16)
    score = jnp.concatenate(
        [
            total(half + tile * QROWS, QROWS) + total(half + (tiles + tile) * QROWS, QROWS)
            for tile in range(tiles)
        ],
        axis=1,
    )
    out, lse = attend(score, value)
    fresh = jnp.concatenate([out.astype(bf16), packed_stat(lse)], axis=0)

    at = half + 2 * tiles * QROWS
    cached = [
        (
            got_ref[part, at : at + QROWS].astype(f32),
            stat(got_ref[part, at + QROWS : at + 2 * QROWS]),
        )
        for part in range(parts)
    ]
    query = q_ref[core, head]
    start = pl.multiple_of(head * HD, HD)
    draft_keys = draft_ref[core, :, pl.ds(start, HD)].astype(f32)
    draft_vals = draft_ref[core, :, pl.ds(start + COLS, HD)].astype(f32)
    token = lax.broadcasted_iota(jnp.int32, (QROWS, 1), 0) % DRAFT
    scores = []
    for u in range(DRAFT):
        one = jnp.sum(query.astype(f32) * draft_keys[u : u + 1], axis=-1, keepdims=True) * SCALE
        scores.append(jnp.where(token >= u, one, NEG))
    top = functools.reduce(jnp.maximum, scores)
    weights = [jnp.where(one > 0.5 * NEG, jnp.exp(one - top), 0.0) for one in scores]
    sums = functools.reduce(jnp.add, weights)
    drafted = functools.reduce(
        jnp.add,
        [w.astype(bf16).astype(f32) * draft_vals[u : u + 1] for u, w in enumerate(weights)],
    )
    out, lse = merge([*cached, (drafted / sums, top + jnp.log(sums))])
    kept = jnp.concatenate([out.astype(bf16), packed_stat(lse)], axis=0)

    chunks = out_ref.shape[1]
    for chunk in range(chunks):
        out_ref[role, chunk] = kept
        out_ref[1 - role, chunk] = fresh


def join_kernel(span_ref, got_ref, out_ref):
    role = lax.axis_index("role")
    for row in range(out_ref.shape[0]):
        taken = span_ref[0, 0] == row
        for head in range(KVH):

            def pair(pool, core):
                tile = got_ref.at[pool, head * 2 + core]
                return tile[:QROWS].astype(f32), stat(tile[QROWS:])

            parts = [pair(role, row)]
            for core in range(2):
                out, lse = pair(1 - role, core)
                parts.append((out, jnp.where(taken, lse, NEG)))
            out_ref[row, head] = merge(parts)[0].astype(bf16)


def call(kernel, out_shapes, spaces, scratch=(), flops=0, moved=0):
    return pl.pallas_call(
        kernel,
        out_shape=out_shapes,
        in_specs=[pl.BlockSpec(memory_space=space) for space in spaces],
        out_specs=jax.tree.map(lambda _: pl.BlockSpec(memory_space=pltpu.VMEM), out_shapes),
        scratch_shapes=list(scratch),
        compiler_params=pltpu.CompilerParams(vmem_limit_bytes=24 << 20),
        cost_estimate=pl.CostEstimate(flops=flops, bytes_accessed=moved, transcendentals=0),
    )


V = pltpu.VMEM
S = pltpu.SMEM


def shards(
    prompt_acts, kv_weight, cache_kv, cache_len, block_owner, span_row, draft_query, draft_kv
):
    swap = [(0, 1), (1, 0)]
    core = lax.axis_index("core")
    acts = prompt_acts[0, 0]
    span, width = acts.shape
    half = span // 2
    rows = cache_kv.shape[1]
    n_yx = lax.axis_size("yx")
    struct = jax.ShapeDtypeStruct

    weight2 = lax.ppermute(kv_weight, "core", swap)
    query = draft_query[0].reshape(rows, DRAFT, KVH, GROUP, HD).transpose(0, 2, 3, 1, 4)
    query = query.reshape(rows, KVH, QROWS, HD)
    chosen = lax.dynamic_index_in_dim(query, span_row[0, 0], 0, keepdims=False)
    asked = lax.ppermute(chosen, "role", swap)
    acts2 = lax.ppermute(
        lax.dynamic_slice_in_dim(acts, (1 - core) * half, half, 0), "core", swap
    )

    block = struct((KVH, 2 * QROWS, HD), bf16)
    mine, other = call(
        cache_kernel, [block, block], [S, S, V, V], flops=400_000_000, moved=2_000_000
    )(block_owner[0], cache_len, query, cache_kv[0])
    theirs = lax.ppermute(other, "core", swap)

    length = half + 2 * (half // HD) * QROWS + 2 * QROWS
    sent = call(
        project_kernel,
        struct((KVH, length, HD), bf16),
        [V] * 7,
        [V((2, KVH * QROWS, width), bf16)],
        flops=1_700_000_000,
        moved=8_000_000,
    )(acts, acts2, kv_weight, weight2, asked, mine, theirs)
    got = lax.all_to_all(sent, "yx", 0, 0, tiled=True)

    parts = call(
        span_kernel,
        struct((2, 2 * n_yx, 2 * QROWS, HD), bf16),
        [V, V, V],
        flops=20_000_000,
        moved=3_000_000,
    )(got, query, draft_kv[0])
    parts = lax.all_to_all(
        parts.reshape(4 * n_yx, 2 * QROWS, HD), ("role", "yx", "core"), 0, 0, tiled=True
    )
    joined = call(
        join_kernel, struct((rows, KVH, QROWS, HD), bf16), [S, V], flops=10_000_000, moved=700_000
    )(span_row, parts.reshape(2, 2 * n_yx, 2 * QROWS, HD))
    output = joined.reshape(rows, KVH, GROUP, DRAFT, HD).transpose(0, 3, 1, 2, 4)
    return output.reshape(1, rows, DRAFT, QH * HD)


def solution(mesh):
    roles, groups, tps = mesh.devices.shape
    fine = Mesh(mesh.devices.reshape(roles, groups, tps // 2, 2), ("role", "grp", "yx", "core"))
    tp = ("yx", "core")
    placed = (
        P("role", "grp", None, tp),
        P(tp, None),
        P("role", "grp", tp, None),
        P("role", "grp"),
        P("role", "grp", None),
        P("role", "grp"),
        P("role", "grp", None, None),
        P("role", "grp", None, None),
    )
    return jax.shard_map(
        shards, mesh=fine, in_specs=placed, out_specs=P("role", "grp", None, None), check_vma=False
    )
```

```python
import functools
import math

import jax
import jax.numpy as jnp
from jax import lax
from jax.experimental import pallas as pl
from jax.experimental.pallas import tpu as pltpu
from jax.sharding import Mesh
from jax.sharding import PartitionSpec as P

QH = 64
KVH = 8
HD = 128
DRAFT = 4
GROUP = QH // KVH
QROWS = GROUP * DRAFT
COLS = KVH * HD
NEG = -1e30
SCALE = 1.0 / math.sqrt(HD)

f32 = jnp.float32
bf16 = jnp.bfloat16


def dot_nt(a, b):
    return lax.dot_general(a, b, (((1,), (1,)), ((), ())), preferred_element_type=f32)


def dot_nn(a, b):
    return jnp.dot(a, b, preferred_element_type=f32)


def packed_stat(lse):
    hi = lse.astype(bf16).astype(f32)
    mid = (lse - hi).astype(bf16).astype(f32)
    lo = lse - hi - mid
    lane = lax.broadcasted_iota(jnp.int32, (lse.shape[0], HD), 1)
    return jnp.where(
        lane == 0, hi, jnp.where(lane == 1, mid, jnp.where(lane == 2, lo, 0.0))
    ).astype(bf16)


def stat(tile):
    return jnp.sum(tile.astype(f32), axis=-1, keepdims=True)


def attend(score, value):
    top = jnp.max(score, axis=-1, keepdims=True)
    weight = jnp.where(score > 0.5 * NEG, jnp.exp(score - top), 0.0)
    total = jnp.sum(weight, axis=-1, keepdims=True)
    any_key = total > 0.0
    safe = jnp.where(any_key, total, 1.0)
    out = dot_nn(weight.astype(bf16), value) / safe
    return out, jnp.where(any_key, top + jnp.log(safe), NEG)


def merge(parts):
    top = functools.reduce(jnp.maximum, [lse for _, lse in parts])
    weights = [jnp.where(lse > 0.5 * NEG, jnp.exp(lse - top), 0.0) for _, lse in parts]
    total = functools.reduce(jnp.add, weights)
    safe = jnp.where(total > 0.0, total, 1.0)
    out = functools.reduce(jnp.add, [w * o for w, (o, _) in zip(weights, parts)])
    return out / safe, jnp.where(total > 0.0, top + jnp.log(safe), NEG)


def stacked(parts):
    return jnp.concatenate(parts, axis=0)


def head_cols(head, start=0):
    return slice(start + head * HD, start + (head + 1) * HD)


def put_pair(out_ref, start, out, lse):
    shape = (KVH, QROWS, HD)
    out_ref[:, start : start + QROWS] = out.astype(bf16).reshape(shape)
    out_ref[:, start + QROWS : start + 2 * QROWS] = packed_stat(lse).reshape(shape)


def cache_kernel(
    owner_hbm, len_hbm, q_ref, cache_hbm, mine_ref, other_ref, owner_ref, len_ref, cache_ref, sems
):
    core = lax.axis_index("core")
    me = lax.axis_index("yx") * 2 + core
    slab = cache_ref.shape[1]
    order = (1 - core, core)
    ints = [
        pltpu.make_async_copy(owner_hbm, owner_ref, sems.at[0]),
        pltpu.make_async_copy(len_hbm, len_ref, sems.at[1]),
    ]
    loads = [
        pltpu.make_async_copy(cache_hbm.at[row], cache_ref.at[k], sems.at[2 + k])
        for k, row in enumerate(order)
    ]
    for copy in (*ints, *loads):
        copy.start()
    for copy in ints:
        copy.wait()
    for k, (row, out_ref) in enumerate(zip(order, (other_ref, mine_ref))):
        first = jnp.int32(0)
        for block in range(owner_ref.shape[1]):
            first = first + jnp.where(owner_ref[row, block] == me, block, 0)
        room = len_ref[0, row] - first * slab
        live = lax.broadcasted_iota(jnp.int32, (KVH * QROWS, slab), 1) < room
        loads[k].wait()
        score = stacked(
            [dot_nt(q_ref[row, head], cache_ref[k, :, head_cols(head)]) for head in range(KVH)]
        )
        score = jnp.where(live, score * SCALE, NEG)
        top = jnp.max(score, axis=-1, keepdims=True)
        weight = jnp.where(live, jnp.exp(score - top), 0.0)
        total = jnp.sum(weight, axis=-1, keepdims=True)
        safe = jnp.where(total > 0.0, total, 1.0)
        weight = weight.astype(bf16)
        out = stacked(
            [
                dot_nn(
                    weight[head * QROWS : (head + 1) * QROWS],
                    cache_ref[k, :, head_cols(head, COLS)],
                )
                for head in range(KVH)
            ]
        )
        put_pair(out_ref, 0, out / safe, jnp.where(total > 0.0, top + jnp.log(safe), NEG))


def project_kernel(
    acts_hbm,
    acts2_hbm,
    w_hbm,
    w2_hbm,
    q_ref,
    mine_ref,
    theirs_ref,
    out_ref,
    acts_ref,
    w_ref,
    qw_ref,
    sems,
):
    core = lax.axis_index("core")
    half = acts_ref.shape[1]
    mine = pl.ds(pl.multiple_of(core * half, half), half)
    keys, values = slice(0, COLS), slice(COLS, 2 * COLS)
    loads = [
        pltpu.make_async_copy(source.at[rows, cols], held.at[k, :, cols], sems.at[number])
        for number, (source, rows, cols, held, k) in enumerate(
            [
                (w_hbm, slice(None), keys, w_ref, 0),
                (w2_hbm, slice(None), keys, w_ref, 1),
                (acts_hbm, mine, slice(None), acts_ref, 0),
                (acts2_hbm, mine, slice(None), acts_ref, 1),
                (w_hbm, slice(None), values, w_ref, 0),
                (w2_hbm, slice(None), values, w_ref, 1),
            ]
        )
    ]
    for copy in loads:
        copy.start()
    for k in range(2):
        loads[k].wait()
        for head in range(KVH):
            rows = slice(head * QROWS, (head + 1) * QROWS)
            qw_ref[k, rows] = dot_nt(q_ref[head], w_ref[k, :, head_cols(head)]).astype(bf16)
    for copy in loads[2:4]:
        copy.wait()
    score = (dot_nt(qw_ref[0], acts_ref[0]) + dot_nt(qw_ref[1], acts_ref[1])) * SCALE
    high = score.astype(bf16)
    low = (score - high.astype(f32)).astype(bf16)
    tiles = half // HD
    for tile in range(tiles):
        for part, words in enumerate((high, low)):
            at = half + (part * tiles + tile) * QROWS
            out_ref[:, at : at + QROWS] = words[:, head_cols(tile)].reshape(KVH, QROWS, HD)
    for copy in loads[4:]:
        copy.wait()
    value = dot_nn(acts_ref[0], w_ref[0, :, values]) + dot_nn(acts_ref[1], w_ref[1, :, values])
    value = value.astype(bf16)
    for head in range(KVH):
        out_ref[head, :half] = value[:, head_cols(head)]
    shape = (KVH * QROWS, HD)
    out, lse = merge(
        [
            (
                ref[:, :QROWS].reshape(shape).astype(f32),
                stat(ref[:, QROWS:].reshape(shape)),
            )
            for ref in (mine_ref, theirs_ref)
        ]
    )
    put_pair(out_ref, half + 2 * tiles * QROWS, out, lse)


def span_kernel(got_ref, q_ref, draft_ref, out_ref):
    parts, length, _ = got_ref.shape
    half = (length - 2 * QROWS) * HD // (HD + 2 * QROWS)
    tiles = half // HD
    role = lax.axis_index("role")
    core = lax.axis_index("core")
    head = lax.axis_index("yx")

    def total(start, size):
        acc = got_ref[0, start : start + size].astype(f32)
        for part in range(1, parts):
            acc = acc + got_ref[part, start : start + size].astype(f32)
        return acc

    value = total(0, half).astype(bf16)
    score = jnp.concatenate(
        [
            total(half + tile * QROWS, QROWS) + total(half + (tiles + tile) * QROWS, QROWS)
            for tile in range(tiles)
        ],
        axis=1,
    )
    out, lse = attend(score, value)
    fresh = jnp.concatenate([out.astype(bf16), packed_stat(lse)], axis=0)

    at = half + 2 * tiles * QROWS
    cached = [
        (
            got_ref[part, at : at + QROWS].astype(f32),
            stat(got_ref[part, at + QROWS : at + 2 * QROWS]),
        )
        for part in range(parts)
    ]
    query = q_ref[core, head]
    start = pl.multiple_of(head * HD, HD)
    draft_keys = draft_ref[core, :, pl.ds(start, HD)].astype(f32)
    draft_vals = draft_ref[core, :, pl.ds(start + COLS, HD)].astype(f32)
    token = lax.broadcasted_iota(jnp.int32, (QROWS, 1), 0) % DRAFT
    scores = []
    for u in range(DRAFT):
        one = jnp.sum(query.astype(f32) * draft_keys[u : u + 1], axis=-1, keepdims=True) * SCALE
        scores.append(jnp.where(token >= u, one, NEG))
    top = functools.reduce(jnp.maximum, scores)
    weights = [jnp.where(one > 0.5 * NEG, jnp.exp(one - top), 0.0) for one in scores]
    sums = functools.reduce(jnp.add, weights)
    drafted = functools.reduce(
        jnp.add,
        [w.astype(bf16).astype(f32) * draft_vals[u : u + 1] for u, w in enumerate(weights)],
    )
    out, lse = merge([*cached, (drafted / sums, top + jnp.log(sums))])
    kept = jnp.concatenate([out.astype(bf16), packed_stat(lse)], axis=0)

    chunks = out_ref.shape[1]
    for chunk in range(chunks):
        out_ref[role, chunk] = kept
        out_ref[1 - role, chunk] = fresh


def join_kernel(span_ref, got_ref, out_ref):
    role = lax.axis_index("role")
    for row in range(out_ref.shape[0]):
        taken = span_ref[0, 0] == row
        for head in range(KVH):

            def pair(pool, core):
                tile = got_ref.at[pool, head * 2 + core]
                return tile[:QROWS].astype(f32), stat(tile[QROWS:])

            parts = [pair(role, row)]
            for core in range(2):
                out, lse = pair(1 - role, core)
                parts.append((out, jnp.where(taken, lse, NEG)))
            out_ref[row, head] = merge(parts)[0].astype(bf16)


def call(kernel, out_shapes, spaces, scratch=(), flops=0, moved=0, limit=24):
    return pl.pallas_call(
        kernel,
        out_shape=out_shapes,
        in_specs=[pl.BlockSpec(memory_space=space) for space in spaces],
        out_specs=jax.tree.map(lambda _: pl.BlockSpec(memory_space=pltpu.VMEM), out_shapes),
        scratch_shapes=list(scratch),
        compiler_params=pltpu.CompilerParams(vmem_limit_bytes=limit << 20),
        cost_estimate=pl.CostEstimate(flops=flops, bytes_accessed=moved, transcendentals=0),
    )


V = pltpu.VMEM
S = pltpu.SMEM
H = pltpu.HBM


def shards(
    prompt_acts, kv_weight, cache_kv, cache_len, block_owner, span_row, draft_query, draft_kv
):
    swap = [(0, 1), (1, 0)]
    acts = prompt_acts[0, 0]
    span, width = acts.shape
    half = span // 2
    rows = cache_kv.shape[1]
    n_yx = lax.axis_size("yx")
    struct = jax.ShapeDtypeStruct

    query = draft_query[0].reshape(rows, DRAFT, KVH, GROUP, HD).transpose(0, 2, 3, 1, 4)
    query = query.reshape(rows, KVH, QROWS, HD)
    chosen = lax.dynamic_index_in_dim(query, span_row[0, 0], 0, keepdims=False)
    asked = lax.ppermute(chosen, "role", swap)
    weight2 = lax.ppermute(kv_weight, "core", swap)
    acts2 = lax.ppermute(acts, "core", swap)

    block = struct((KVH, 2 * QROWS, HD), bf16)
    mine, other = call(
        cache_kernel,
        [block, block],
        [H, H, V, H],
        [
            S(block_owner.shape[1:], jnp.int32),
            S(cache_len.shape, jnp.int32),
            V(cache_kv.shape[1:], bf16),
            pltpu.SemaphoreType.DMA((4,)),
        ],
        flops=400_000_000,
        moved=2_000_000,
        limit=58,
    )(block_owner[0], cache_len, query, cache_kv[0])
    asked, other = lax.optimization_barrier((asked, other))
    theirs = lax.ppermute(other, "core", swap)

    length = half + 2 * (half // HD) * QROWS + 2 * QROWS
    sent = call(
        project_kernel,
        struct((KVH, length, HD), bf16),
        [H, H, H, H, V, V, V],
        [
            V((2, half, width), bf16),
            V((2, *kv_weight.shape), bf16),
            V((2, KVH * QROWS, width), bf16),
            pltpu.SemaphoreType.DMA((6,)),
        ],
        flops=1_700_000_000,
        moved=8_000_000,
        limit=50,
    )(acts, acts2, kv_weight, weight2, asked, mine, theirs)
    got = lax.all_to_all(sent, "yx", 0, 0, tiled=True)

    parts = call(
        span_kernel,
        struct((2, 2 * n_yx, 2 * QROWS, HD), bf16),
        [V, V, V],
        flops=20_000_000,
        moved=3_000_000,
    )(got, query, draft_kv[0])
    parts = lax.all_to_all(
        parts.reshape(4 * n_yx, 2 * QROWS, HD), ("role", "yx", "core"), 0, 0, tiled=True
    )
    joined = call(
        join_kernel, struct((rows, KVH, QROWS, HD), bf16), [S, V], flops=10_000_000, moved=700_000
    )(span_row, parts.reshape(2, 2 * n_yx, 2 * QROWS, HD))
    output = joined.reshape(rows, KVH, GROUP, DRAFT, HD).transpose(0, 3, 1, 2, 4)
    return output.reshape(1, rows, DRAFT, QH * HD)


def solution(mesh):
    roles, groups, tps = mesh.devices.shape
    fine = Mesh(mesh.devices.reshape(roles, groups, tps // 2, 2), ("role", "grp", "yx", "core"))
    tp = ("yx", "core")
    placed = (
        P("role", "grp", None, tp),
        P(tp, None),
        P("role", "grp", tp, None),
        P("role", "grp"),
        P("role", "grp", None),
        P("role", "grp"),
        P("role", "grp", None, None),
        P("role", "grp", None, None),
    )
    return jax.shard_map(
        shards, mesh=fine, in_specs=placed, out_specs=P("role", "grp", None, None), check_vma=False
    )
```

```python
import functools
import math

import jax
import jax.numpy as jnp
from jax import lax
from jax.experimental import pallas as pl
from jax.experimental.pallas import tpu as pltpu
from jax.sharding import Mesh
from jax.sharding import PartitionSpec as P

QH = 64
KVH = 8
HD = 128
DRAFT = 4
GROUP = QH // KVH
QROWS = GROUP * DRAFT
COLS = KVH * HD
NEG = -1e30
SCALE = 1.0 / math.sqrt(HD)

f32 = jnp.float32
bf16 = jnp.bfloat16


def dot_nt(a, b):
    return lax.dot_general(a, b, (((1,), (1,)), ((), ())), preferred_element_type=f32)


def dot_nn(a, b):
    return jnp.dot(a, b, preferred_element_type=f32)


def packed_stat(lse):
    hi = lse.astype(bf16).astype(f32)
    mid = (lse - hi).astype(bf16).astype(f32)
    lo = lse - hi - mid
    lane = lax.broadcasted_iota(jnp.int32, (lse.shape[0], HD), 1)
    return jnp.where(
        lane == 0, hi, jnp.where(lane == 1, mid, jnp.where(lane == 2, lo, 0.0))
    ).astype(bf16)


def stat(tile):
    return jnp.sum(tile.astype(f32), axis=-1, keepdims=True)


def attend(score, value):
    top = jnp.max(score, axis=-1, keepdims=True)
    weight = jnp.where(score > 0.5 * NEG, jnp.exp(score - top), 0.0)
    total = jnp.sum(weight, axis=-1, keepdims=True)
    any_key = total > 0.0
    safe = jnp.where(any_key, total, 1.0)
    out = dot_nn(weight.astype(bf16), value) / safe
    return out, jnp.where(any_key, top + jnp.log(safe), NEG)


def merge(parts):
    top = functools.reduce(jnp.maximum, [lse for _, lse in parts])
    weights = [jnp.where(lse > 0.5 * NEG, jnp.exp(lse - top), 0.0) for _, lse in parts]
    total = functools.reduce(jnp.add, weights)
    safe = jnp.where(total > 0.0, total, 1.0)
    out = functools.reduce(jnp.add, [w * o for w, (o, _) in zip(weights, parts)])
    return out / safe, jnp.where(total > 0.0, top + jnp.log(safe), NEG)


def stacked(parts):
    return jnp.concatenate(parts, axis=0)


def head_cols(head, start=0):
    return slice(start + head * HD, start + (head + 1) * HD)


def get_pair(tile):
    shape = (tile.shape[0] * QROWS, HD)
    return tile[:, :QROWS].reshape(shape).astype(f32), stat(tile[:, QROWS:].reshape(shape))


def cache_kernel(
    owner_hbm, len_hbm, q_ref, cache_hbm, *refs
):
    out_refs, (owner_ref, len_ref, cache_ref, sems) = refs[:4], refs[4:]
    side = lax.rem(lax.axis_index("yx"), 2)
    core = lax.axis_index("core")
    me = lax.axis_index("yx") * 2 + core
    slab = cache_ref.shape[1]
    order = (1 - core, core)
    ints = [
        pltpu.make_async_copy(owner_hbm, owner_ref, sems.at[0]),
        pltpu.make_async_copy(len_hbm, len_ref, sems.at[1]),
    ]
    loads = [
        pltpu.make_async_copy(cache_hbm.at[row], cache_ref.at[k], sems.at[2 + k])
        for k, row in enumerate(order)
    ]
    for copy in (*ints, *loads):
        copy.start()
    for copy in ints:
        copy.wait()
    for k, row in enumerate(order):
        first = jnp.int32(0)
        for block in range(owner_ref.shape[1]):
            first = first + jnp.where(owner_ref[row, block] == me, block, 0)
        room = len_ref[0, row] - first * slab
        live = lax.broadcasted_iota(jnp.int32, (KVH * QROWS, slab), 1) < room
        loads[k].wait()
        score = stacked(
            [dot_nt(q_ref[row, head], cache_ref[k, :, head_cols(head)]) for head in range(KVH)]
        )
        score = jnp.where(live, score * SCALE, NEG)
        top = jnp.max(score, axis=-1, keepdims=True)
        weight = jnp.where(live, jnp.exp(score - top), 0.0)
        total = jnp.sum(weight, axis=-1, keepdims=True)
        safe = jnp.where(total > 0.0, total, 1.0)
        weight = weight.astype(bf16)
        out = stacked(
            [
                dot_nn(
                    weight[head * QROWS : (head + 1) * QROWS],
                    cache_ref[k, :, head_cols(head, COLS)],
                )
                for head in range(KVH)
            ]
        )
        shape = (KVH, QROWS, HD)
        out = (out / safe).astype(bf16).reshape(shape)
        lse = packed_stat(jnp.where(total > 0.0, top + jnp.log(safe), NEG)).reshape(shape)
        for head in range(KVH):
            near, far = out_refs[1 - k], out_refs[3 - k]

            def put(out_ref, head=head):
                out_ref[head // 2, :QROWS] = out[head]
                out_ref[head // 2, QROWS:] = lse[head]

            pl.when(side == head % 2)(functools.partial(put, near))
            pl.when(side != head % 2)(functools.partial(put, far))


def chip_kernel(a_ref, b_ref, c_ref, d_ref, *out_refs):
    out, lse = merge([get_pair(ref[...]) for ref in (a_ref, b_ref, c_ref, d_ref)])
    shape = (KVH // 2, QROWS, HD)
    out = out.astype(bf16).reshape(shape)
    lse = packed_stat(lse).reshape(shape)
    place = lax.axis_index("yx") // 2
    for head in range(KVH // 2):
        for step, out_ref in enumerate(out_refs):

            def put(head=head, out_ref=out_ref):
                out_ref[0, :QROWS] = out[head]
                out_ref[0, QROWS:] = lse[head]

            pl.when(lax.rem(place + step, KVH // 2) == head)(put)


def project_kernel(
    acts_hbm,
    acts2_hbm,
    w_hbm,
    w2_hbm,
    q_ref,
    out_ref,
    acts_ref,
    w_ref,
    qw_ref,
    sems,
):
    core = lax.axis_index("core")
    half = acts_ref.shape[1]
    mine = pl.ds(pl.multiple_of(core * half, half), half)
    keys, values = slice(0, COLS), slice(COLS, 2 * COLS)
    loads = [
        pltpu.make_async_copy(source.at[rows, cols], held.at[k, :, cols], sems.at[number])
        for number, (source, rows, cols, held, k) in enumerate(
            [
                (w_hbm, slice(None), keys, w_ref, 0),
                (w2_hbm, slice(None), keys, w_ref, 1),
                (acts_hbm, mine, slice(None), acts_ref, 0),
                (acts2_hbm, mine, slice(None), acts_ref, 1),
                (w_hbm, slice(None), values, w_ref, 0),
                (w2_hbm, slice(None), values, w_ref, 1),
            ]
        )
    ]
    for copy in loads:
        copy.start()
    for k in range(2):
        loads[k].wait()
        for head in range(KVH):
            rows = slice(head * QROWS, (head + 1) * QROWS)
            qw_ref[k, rows] = dot_nt(q_ref[head], w_ref[k, :, head_cols(head)]).astype(bf16)
    for copy in loads[2:4]:
        copy.wait()
    score = (dot_nt(qw_ref[0], acts_ref[0]) + dot_nt(qw_ref[1], acts_ref[1])) * SCALE
    score = score.astype(bf16)
    for tile in range(half // HD):
        at = half + tile * QROWS
        out_ref[:, at : at + QROWS] = score[:, head_cols(tile)].reshape(KVH, QROWS, HD)
    for copy in loads[4:]:
        copy.wait()
    value = dot_nn(acts_ref[0], w_ref[0, :, values]) + dot_nn(acts_ref[1], w_ref[1, :, values])
    value = value.astype(bf16)
    for head in range(KVH):
        out_ref[head, :half] = value[:, head_cols(head)]


def span_kernel(got_ref, q_ref, draft_ref, a_ref, b_ref, c_ref, d_ref, out_ref):
    parts, length, _ = got_ref.shape
    half = length * HD // (HD + QROWS)
    tiles = half // HD
    role = lax.axis_index("role")
    core = lax.axis_index("core")
    head = lax.axis_index("yx")

    def total(start, size):
        acc = got_ref[0, start : start + size].astype(f32)
        for part in range(1, parts):
            acc = acc + got_ref[part, start : start + size].astype(f32)
        return acc

    value = total(0, half).astype(bf16)
    score = jnp.concatenate(
        [total(half + tile * QROWS, QROWS) for tile in range(tiles)], axis=1
    )
    out, lse = attend(score, value)
    fresh = jnp.concatenate([out.astype(bf16), packed_stat(lse)], axis=0)

    cached = [get_pair(ref[...]) for ref in (a_ref, b_ref, c_ref, d_ref)]
    query = q_ref[core, head]
    start = pl.multiple_of(head * HD, HD)
    draft_keys = draft_ref[core, :, pl.ds(start, HD)].astype(f32)
    draft_vals = draft_ref[core, :, pl.ds(start + COLS, HD)].astype(f32)
    token = lax.broadcasted_iota(jnp.int32, (QROWS, 1), 0) % DRAFT
    scores = []
    for u in range(DRAFT):
        one = jnp.sum(query.astype(f32) * draft_keys[u : u + 1], axis=-1, keepdims=True) * SCALE
        scores.append(jnp.where(token >= u, one, NEG))
    top = functools.reduce(jnp.maximum, scores)
    weights = [jnp.where(one > 0.5 * NEG, jnp.exp(one - top), 0.0) for one in scores]
    sums = functools.reduce(jnp.add, weights)
    drafted = functools.reduce(
        jnp.add,
        [w.astype(bf16).astype(f32) * draft_vals[u : u + 1] for u, w in enumerate(weights)],
    )
    out, lse = merge([*cached, (drafted / sums, top + jnp.log(sums))])
    kept = jnp.concatenate([out.astype(bf16), packed_stat(lse)], axis=0)

    chunks = out_ref.shape[1]
    for chunk in range(chunks):
        out_ref[role, chunk] = kept
        out_ref[1 - role, chunk] = fresh


def join_kernel(span_ref, got_ref, out_ref):
    role = lax.axis_index("role")
    for row in range(out_ref.shape[0]):
        taken = span_ref[0, 0] == row
        for head in range(KVH):

            def pair(pool, core):
                tile = got_ref.at[pool, head * 2 + core]
                return tile[:QROWS].astype(f32), stat(tile[QROWS:])

            parts = [pair(role, row)]
            for core in range(2):
                out, lse = pair(1 - role, core)
                parts.append((out, jnp.where(taken, lse, NEG)))
            out_ref[row, head] = merge(parts)[0].astype(bf16)


def call(kernel, out_shapes, spaces, scratch=(), flops=0, moved=0, limit=24):
    return pl.pallas_call(
        kernel,
        out_shape=out_shapes,
        in_specs=[pl.BlockSpec(memory_space=space) for space in spaces],
        out_specs=jax.tree.map(lambda _: pl.BlockSpec(memory_space=pltpu.VMEM), out_shapes),
        scratch_shapes=list(scratch),
        compiler_params=pltpu.CompilerParams(vmem_limit_bytes=limit << 20),
        cost_estimate=pl.CostEstimate(flops=flops, bytes_accessed=moved, transcendentals=0),
    )


V = pltpu.VMEM
S = pltpu.SMEM
H = pltpu.HBM


def shards(
    prompt_acts, kv_weight, cache_kv, cache_len, block_owner, span_row, draft_query, draft_kv
):
    swap = [(0, 1), (1, 0)]
    acts = prompt_acts[0, 0]
    span, width = acts.shape
    half = span // 2
    rows = cache_kv.shape[1]
    n_yx = lax.axis_size("yx")
    struct = jax.ShapeDtypeStruct

    query = draft_query[0].reshape(rows, DRAFT, KVH, GROUP, HD).transpose(0, 2, 3, 1, 4)
    query = query.reshape(rows, KVH, QROWS, HD)
    chosen = lax.dynamic_index_in_dim(query, span_row[0, 0], 0, keepdims=False)
    asked = lax.ppermute(chosen, "role", swap)
    weight2 = lax.ppermute(kv_weight, "core", swap)
    acts2 = lax.ppermute(acts, "core", swap)

    tp = ("yx", "core")

    def apart(x, flip):
        return lax.ppermute(x, tp, [(i, i ^ flip) for i in range(2 * n_yx)])

    def along(x, step):
        return lax.ppermute(x, tp, [(i, (i + 4 * step) % (2 * n_yx)) for i in range(2 * n_yx)])

    pieces = call(
        cache_kernel,
        [struct((KVH // 2, 2 * QROWS, HD), bf16)] * 4,
        [H, H, V, H],
        [
            S(block_owner.shape[1:], jnp.int32),
            S(cache_len.shape, jnp.int32),
            V(cache_kv.shape[1:], bf16),
            pltpu.SemaphoreType.DMA((4,)),
        ],
        flops=400_000_000,
        moved=2_000_000,
        limit=58,
    )(block_owner[0], cache_len, query, cache_kv[0])
    asked, pieces = lax.optimization_barrier((asked, pieces))

    length = half + (half // HD) * QROWS
    sent = call(
        project_kernel,
        struct((KVH, length, HD), bf16),
        [H, H, H, H, V],
        [
            V((2, half, width), bf16),
            V((2, *kv_weight.shape), bf16),
            V((2, KVH * QROWS, width), bf16),
            pltpu.SemaphoreType.DMA((6,)),
        ],
        flops=1_700_000_000,
        moved=8_000_000,
        limit=50,
    )(acts, acts2, kv_weight, weight2, asked)
    sent, pieces = lax.optimization_barrier((sent, pieces))
    got = lax.all_to_all(sent, "yx", 0, 0, tiled=True)
    pieces = [pieces[0]] + [apart(pieces[flip], flip) for flip in (1, 2, 3)]
    pieces = call(
        chip_kernel,
        [struct((1, 2 * QROWS, HD), bf16)] * (n_yx // 2),
        [V] * 4,
        flops=10_000_000,
        moved=400_000,
    )(*pieces)
    pieces = [pieces[0]] + [along(pieces[step], step) for step in range(1, n_yx // 2)]

    parts = call(
        span_kernel,
        struct((2, 2 * n_yx, 2 * QROWS, HD), bf16),
        [V] * 7,
        flops=20_000_000,
        moved=3_000_000,
    )(got, query, draft_kv[0], *pieces)
    parts = lax.all_to_all(
        parts.reshape(4 * n_yx, 2 * QROWS, HD), ("role", "yx", "core"), 0, 0, tiled=True
    )
    joined = call(
        join_kernel, struct((rows, KVH, QROWS, HD), bf16), [S, V], flops=10_000_000, moved=700_000
    )(span_row, parts.reshape(2, 2 * n_yx, 2 * QROWS, HD))
    output = joined.reshape(rows, KVH, GROUP, DRAFT, HD).transpose(0, 3, 1, 2, 4)
    return output.reshape(1, rows, DRAFT, QH * HD)


def solution(mesh):
    roles, groups, tps = mesh.devices.shape
    fine = Mesh(mesh.devices.reshape(roles, groups, tps // 2, 2), ("role", "grp", "yx", "core"))
    tp = ("yx", "core")
    placed = (
        P("role", "grp", None, tp),
        P(tp, None),
        P("role", "grp", tp, None),
        P("role", "grp"),
        P("role", "grp", None),
        P("role", "grp"),
        P("role", "grp", None, None),
        P("role", "grp", None, None),
    )
    return jax.shard_map(
        shards, mesh=fine, in_specs=placed, out_specs=P("role", "grp", None, None), check_vma=False
    )
```

```python
import functools
import math

import jax
import jax.numpy as jnp
from jax import lax
from jax.experimental import pallas as pl
from jax.experimental.pallas import tpu as pltpu
from jax.sharding import Mesh
from jax.sharding import PartitionSpec as P

QH = 64
KVH = 8
HD = 128
DRAFT = 4
GROUP = QH // KVH
QROWS = GROUP * DRAFT
COLS = KVH * HD
NEG = -1e30
SCALE = 1.0 / math.sqrt(HD)

f32 = jnp.float32
bf16 = jnp.bfloat16


def dot_nt(a, b):
    return lax.dot_general(a, b, (((1,), (1,)), ((), ())), preferred_element_type=f32)


def dot_nn(a, b):
    return jnp.dot(a, b, preferred_element_type=f32)


def packed_stat(lse):
    hi = lse.astype(bf16).astype(f32)
    mid = (lse - hi).astype(bf16).astype(f32)
    lo = lse - hi - mid
    lane = lax.broadcasted_iota(jnp.int32, (lse.shape[0], HD), 1)
    return jnp.where(
        lane == 0, hi, jnp.where(lane == 1, mid, jnp.where(lane == 2, lo, 0.0))
    ).astype(bf16)


def stat(tile):
    return jnp.sum(tile.astype(f32), axis=-1, keepdims=True)


def attend(score, value):
    top = jnp.max(score, axis=-1, keepdims=True)
    weight = jnp.where(score > 0.5 * NEG, jnp.exp(score - top), 0.0)
    total = jnp.sum(weight, axis=-1, keepdims=True)
    any_key = total > 0.0
    safe = jnp.where(any_key, total, 1.0)
    out = dot_nn(weight.astype(bf16), value) / safe
    return out, jnp.where(any_key, top + jnp.log(safe), NEG)


def merge(parts):
    top = functools.reduce(jnp.maximum, [lse for _, lse in parts])
    weights = [jnp.where(lse > 0.5 * NEG, jnp.exp(lse - top), 0.0) for _, lse in parts]
    total = functools.reduce(jnp.add, weights)
    safe = jnp.where(total > 0.0, total, 1.0)
    out = functools.reduce(jnp.add, [w * o for w, (o, _) in zip(weights, parts)])
    return out / safe, jnp.where(total > 0.0, top + jnp.log(safe), NEG)


def stacked(parts):
    return jnp.concatenate(parts, axis=0)


def head_cols(head, start=0):
    return slice(start + head * HD, start + (head + 1) * HD)


def put_pair(out_ref, start, out, lse):
    shape = (KVH, QROWS, HD)
    out_ref[:, start : start + QROWS] = out.astype(bf16).reshape(shape)
    out_ref[:, start + QROWS : start + 2 * QROWS] = packed_stat(lse).reshape(shape)


def get_pair(ref, start):
    shape = (KVH * QROWS, HD)
    middle = start + QROWS
    return (
        ref[:, start:middle].reshape(shape).astype(f32),
        stat(ref[:, middle : middle + QROWS].reshape(shape)),
    )


def front_kernel(
    owner_hbm,
    len_hbm,
    q_hbm,
    cache_hbm,
    acts_hbm,
    w_hbm,
    away_ref,
    value_ref,
    mine_ref,
    owner_ref,
    len_ref,
    q_ref,
    cache_ref,
    acts_ref,
    w_ref,
    sems,
):
    core = lax.axis_index("core")
    me = lax.axis_index("yx") * 2 + core
    slab = cache_ref.shape[1]
    span = acts_ref.shape[0]
    half = span // 2
    order = (1 - core, core)
    ints = [
        pltpu.make_async_copy(owner_hbm, owner_ref, sems.at[0]),
        pltpu.make_async_copy(len_hbm, len_ref, sems.at[1]),
        pltpu.make_async_copy(q_hbm, q_ref, sems.at[2]),
    ]
    loads = [
        pltpu.make_async_copy(cache_hbm.at[row], cache_ref.at[k], sems.at[3 + k])
        for k, row in enumerate(order)
    ]
    late = [
        pltpu.make_async_copy(acts_hbm, acts_ref, sems.at[5]),
        pltpu.make_async_copy(w_hbm.at[:, COLS : 2 * COLS], w_ref, sems.at[6]),
    ]
    for copy in (*ints, *loads, *late):
        copy.start()
    for copy in ints:
        copy.wait()
    for k, row in enumerate(order):
        first = jnp.int32(0)
        for block in range(owner_ref.shape[1]):
            first = first + jnp.where(owner_ref[row, block] == me, block, 0)
        room = len_ref[0, row] - first * slab
        live = lax.broadcasted_iota(jnp.int32, (KVH * QROWS, slab), 1) < room
        loads[k].wait()
        score = stacked(
            [dot_nt(q_ref[row, head], cache_ref[k, :, head_cols(head)]) for head in range(KVH)]
        )
        score = jnp.where(live, score * SCALE, NEG)
        top = jnp.max(score, axis=-1, keepdims=True)
        weight = jnp.where(live, jnp.exp(score - top), 0.0)
        total = jnp.sum(weight, axis=-1, keepdims=True)
        safe = jnp.where(total > 0.0, total, 1.0)
        weight = weight.astype(bf16)
        out = stacked(
            [
                dot_nn(
                    weight[head * QROWS : (head + 1) * QROWS],
                    cache_ref[k, :, head_cols(head, COLS)],
                )
                for head in range(KVH)
            ]
        )
        lse = jnp.where(total > 0.0, top + jnp.log(safe), NEG)
        if k == 0:
            put_pair(away_ref, half, out / safe, lse)
        else:
            put_pair(mine_ref, 0, out / safe, lse)
    for copy in late:
        copy.wait()
    for row, out_ref in zip(order, (away_ref, value_ref)):
        tokens = acts_ref[pl.ds(pl.multiple_of(row * half, half), half), :]
        value = dot_nn(tokens, w_ref[...]).astype(bf16)
        for head in range(KVH):
            out_ref[head, :half] = value[:, head_cols(head)]


def score_kernel(
    q_ref, acts_hbm, w_hbm, _, away_hbm, own_ref, acts_ref, w_ref, qw_ref, words_ref, sems
):
    core = lax.axis_index("core")
    half = acts_ref.shape[0] // 2
    loads = [
        pltpu.make_async_copy(w_hbm.at[:, 0:COLS], w_ref, sems.at[0]),
        pltpu.make_async_copy(acts_hbm, acts_ref, sems.at[1]),
    ]
    for copy in loads:
        copy.start()
    loads[0].wait()
    for head in range(KVH):
        rows = slice(head * QROWS, (head + 1) * QROWS)
        qw_ref[rows] = dot_nt(q_ref[head], w_ref[:, head_cols(head)]).astype(bf16)
    loads[1].wait()
    tiles = half // HD

    def tokens(row):
        return acts_ref[pl.ds(pl.multiple_of(row * half, half), half), :]

    score = dot_nt(qw_ref[...], tokens(1 - core)) * SCALE
    high = score.astype(bf16)
    low = (score - high.astype(f32)).astype(bf16)
    for part, words in enumerate((high, low)):
        for tile in range(tiles):
            at = (part * tiles + tile) * QROWS
            words_ref[:, at : at + QROWS] = words[:, head_cols(tile)].reshape(KVH, QROWS, HD)
    start = half + 2 * QROWS
    store = pltpu.make_async_copy(
        words_ref, away_hbm.at[:, start : start + 2 * tiles * QROWS], sems.at[2]
    )
    store.start()
    own_ref[...] = dot_nt(qw_ref[...], tokens(core)) * SCALE
    store.wait()


def pack_kernel(got_ref, value_ref, own_ref, mine_ref, out_ref):
    half = value_ref.shape[1]
    tiles = half // HD
    out_ref[:, :half] = (value_ref[...].astype(f32) + got_ref[:, :half].astype(f32)).astype(bf16)
    shape = (KVH, QROWS, HD)
    start = half + 2 * QROWS
    for tile in range(tiles):
        score = own_ref[:, head_cols(tile)].reshape(shape)
        for part in range(2):
            at = start + (part * tiles + tile) * QROWS
            score = score + got_ref[:, at : at + QROWS].astype(f32)
        at = half + tile * QROWS
        out_ref[:, at : at + QROWS] = score.astype(bf16)
    out, lse = merge([get_pair(mine_ref, 0), get_pair(got_ref, half)])
    put_pair(out_ref, half + tiles * QROWS, out, lse)


def span_kernel(got_ref, q_ref, draft_ref, out_ref):
    parts, length, _ = got_ref.shape
    half = (length - 2 * QROWS) * HD // (HD + QROWS)
    tiles = half // HD
    role = lax.axis_index("role")
    core = lax.axis_index("core")
    head = lax.axis_index("yx")

    def total(start, size):
        acc = got_ref[0, start : start + size].astype(f32)
        for part in range(1, parts):
            acc = acc + got_ref[part, start : start + size].astype(f32)
        return acc

    value = total(0, half).astype(bf16)
    score = jnp.concatenate(
        [total(half + tile * QROWS, QROWS) for tile in range(tiles)], axis=1
    )
    out, lse = attend(score, value)
    fresh = jnp.concatenate([out.astype(bf16), packed_stat(lse)], axis=0)

    at = half + tiles * QROWS
    cached = [
        (
            got_ref[part, at : at + QROWS].astype(f32),
            stat(got_ref[part, at + QROWS : at + 2 * QROWS]),
        )
        for part in range(parts)
    ]
    query = q_ref[core, head]
    start = pl.multiple_of(head * HD, HD)
    draft_keys = draft_ref[core, :, pl.ds(start, HD)].astype(f32)
    draft_vals = draft_ref[core, :, pl.ds(start + COLS, HD)].astype(f32)
    token = lax.broadcasted_iota(jnp.int32, (QROWS, 1), 0) % DRAFT
    scores = []
    for u in range(DRAFT):
        one = jnp.sum(query.astype(f32) * draft_keys[u : u + 1], axis=-1, keepdims=True) * SCALE
        scores.append(jnp.where(token >= u, one, NEG))
    top = functools.reduce(jnp.maximum, scores)
    weights = [jnp.where(one > 0.5 * NEG, jnp.exp(one - top), 0.0) for one in scores]
    sums = functools.reduce(jnp.add, weights)
    drafted = functools.reduce(
        jnp.add,
        [w.astype(bf16).astype(f32) * draft_vals[u : u + 1] for u, w in enumerate(weights)],
    )
    out, lse = merge([*cached, (drafted / sums, top + jnp.log(sums))])
    kept = jnp.concatenate([out.astype(bf16), packed_stat(lse)], axis=0)

    chunks = out_ref.shape[1]
    for chunk in range(chunks):
        out_ref[role, chunk] = kept
        out_ref[1 - role, chunk] = fresh


def join_kernel(span_ref, got_ref, out_ref):
    role = lax.axis_index("role")
    for row in range(out_ref.shape[0]):
        taken = span_ref[0, 0] == row
        for head in range(KVH):

            def pair(pool, core):
                tile = got_ref.at[pool, head * 2 + core]
                return tile[:QROWS].astype(f32), stat(tile[QROWS:])

            parts = [pair(role, row)]
            for core in range(2):
                out, lse = pair(1 - role, core)
                parts.append((out, jnp.where(taken, lse, NEG)))
            out_ref[row, head] = merge(parts)[0].astype(bf16)


def call(kernel, out_shapes, spaces, scratch=(), flops=0, moved=0, limit=24, aliases=None):
    out_specs = jax.tree.map(lambda _: pl.BlockSpec(memory_space=pltpu.VMEM), out_shapes)
    for target in (aliases or {}).values():
        out_specs[target] = pl.BlockSpec(memory_space=H)
    return pl.pallas_call(
        kernel,
        out_shape=out_shapes,
        in_specs=[pl.BlockSpec(memory_space=space) for space in spaces],
        out_specs=out_specs,
        input_output_aliases=aliases or {},
        scratch_shapes=list(scratch),
        compiler_params=pltpu.CompilerParams(vmem_limit_bytes=limit << 20),
        cost_estimate=pl.CostEstimate(flops=flops, bytes_accessed=moved, transcendentals=0),
    )


V = pltpu.VMEM
S = pltpu.SMEM
H = pltpu.HBM
FRONT = 58
SCORE = 52


def shards(
    prompt_acts, kv_weight, cache_kv, cache_len, block_owner, span_row, draft_query, draft_kv
):
    swap = [(0, 1), (1, 0)]
    acts = prompt_acts[0, 0]
    span, width = acts.shape
    half = span // 2
    rows = cache_kv.shape[1]
    n_yx = lax.axis_size("yx")
    struct = jax.ShapeDtypeStruct

    query = draft_query[0].reshape(rows, DRAFT, KVH, GROUP, HD).transpose(0, 2, 3, 1, 4)
    query = query.reshape(rows, KVH, QROWS, HD)
    chosen = lax.dynamic_index_in_dim(query, span_row[0, 0], 0, keepdims=False)
    asked = lax.ppermute(chosen, "role", swap)

    dma = pltpu.SemaphoreType.DMA
    words = 2 * (half // HD) * QROWS
    away = struct((KVH, half + 2 * QROWS + words, HD), bf16)
    away, value, mine = call(
        front_kernel,
        [away, struct((KVH, half, HD), bf16), struct((KVH, 2 * QROWS, HD), bf16)],
        [H] * 6,
        [
            S(block_owner.shape[1:], jnp.int32),
            S(cache_len.shape, jnp.int32),
            V(query.shape, bf16),
            V(cache_kv.shape[1:], bf16),
            V(acts.shape, bf16),
            V((width, COLS), bf16),
            dma((7,)),
        ],
        flops=1_500_000_000,
        moved=6_000_000,
        limit=FRONT,
    )(block_owner[0], cache_len, query, cache_kv[0], acts, kv_weight)
    asked, away = lax.optimization_barrier((asked, away))
    away, own = call(
        score_kernel,
        [struct(away.shape, bf16), struct((KVH * QROWS, half), f32)],
        [V, H, H, H],
        [
            V(acts.shape, bf16),
            V((width, COLS), bf16),
            V((KVH * QROWS, width), bf16),
            V((KVH, words, HD), bf16),
            dma((3,)),
        ],
        flops=600_000_000,
        moved=3_000_000,
        limit=SCORE,
        aliases={3: 0},
    )(asked, acts, kv_weight, away)
    theirs = lax.ppermute(away, "core", swap)
    sent = call(
        pack_kernel,
        struct((KVH, half + (half // HD) * QROWS + 2 * QROWS, HD), bf16),
        [V] * 4,
        flops=10_000_000,
        moved=5_000_000,
    )(theirs, value, own, mine)
    got = lax.all_to_all(sent, "yx", 0, 0, tiled=True)

    parts = call(
        span_kernel,
        struct((2, 2 * n_yx, 2 * QROWS, HD), bf16),
        [V, V, V],
        flops=20_000_000,
        moved=3_000_000,
    )(got, query, draft_kv[0])
    parts = lax.all_to_all(
        parts.reshape(4 * n_yx, 2 * QROWS, HD), ("role", "yx", "core"), 0, 0, tiled=True
    )
    joined = call(
        join_kernel, struct((rows, KVH, QROWS, HD), bf16), [S, V], flops=10_000_000, moved=700_000
    )(span_row, parts.reshape(2, 2 * n_yx, 2 * QROWS, HD))
    output = joined.reshape(rows, KVH, GROUP, DRAFT, HD).transpose(0, 3, 1, 2, 4)
    return output.reshape(1, rows, DRAFT, QH * HD)


def solution(mesh):
    roles, groups, tps = mesh.devices.shape
    fine = Mesh(mesh.devices.reshape(roles, groups, tps // 2, 2), ("role", "grp", "yx", "core"))
    tp = ("yx", "core")
    placed = (
        P("role", "grp", None, tp),
        P(tp, None),
        P("role", "grp", tp, None),
        P("role", "grp"),
        P("role", "grp", None),
        P("role", "grp"),
        P("role", "grp", None, None),
        P("role", "grp", None, None),
    )
    return jax.shard_map(
        shards, mesh=fine, in_specs=placed, out_specs=P("role", "grp", None, None), check_vma=False
    )
```

```python
import functools
import math

import jax
import jax.numpy as jnp
from jax import lax
from jax.experimental import pallas as pl
from jax.experimental.pallas import tpu as pltpu
from jax.sharding import Mesh
from jax.sharding import PartitionSpec as P

QH = 64
KVH = 8
HD = 128
DRAFT = 4
GROUP = QH // KVH
QROWS = GROUP * DRAFT
STAT = 16
PAIR = QROWS + STAT
COLS = KVH * HD
NEG = -1e30
SCALE = 1.0 / math.sqrt(HD)

f32 = jnp.float32
bf16 = jnp.bfloat16


def dot_nt(a, b):
    return lax.dot_general(a, b, (((1,), (1,)), ((), ())), preferred_element_type=f32)


def dot_nn(a, b):
    return jnp.dot(a, b, preferred_element_type=f32)


def terms(lse):
    hi = lse.astype(bf16).astype(f32)
    mid = (lse - hi).astype(bf16).astype(f32)
    return hi, mid, lse - hi - mid


def packed_stat(lse):
    lane = lax.broadcasted_iota(jnp.int32, (QROWS, HD), 1)
    tile = jnp.zeros((QROWS, HD), f32)
    for at, term in enumerate(terms(lse)):
        tile = jnp.where(lane == at, term, tile)
    rows = tile.T[:STAT]
    return jnp.concatenate([rows, jnp.zeros((STAT, HD - QROWS), f32)], axis=1).astype(bf16)


def stat_row(tile):
    rows = tile.astype(f32)
    return rows[0:1] + rows[1:2] + rows[2:3]


def columns(rows):
    count = rows.shape[0]
    square = jnp.concatenate([rows, jnp.zeros((HD - count, HD), f32)], axis=0).T
    return [square[:QROWS, k : k + 1] for k in range(count)]


def attend(score, value):
    top = jnp.max(score, axis=-1, keepdims=True)
    weight = jnp.where(score > 0.5 * NEG, jnp.exp(score - top), 0.0)
    total = jnp.sum(weight, axis=-1, keepdims=True)
    any_key = total > 0.0
    safe = jnp.where(any_key, total, 1.0)
    out = dot_nn(weight.astype(bf16), value) / safe
    return out, jnp.where(any_key, top + jnp.log(safe), NEG)


def shares(rows):
    top = functools.reduce(jnp.maximum, rows)
    weights = [jnp.where(row > 0.5 * NEG, jnp.exp(row - top), 0.0) for row in rows]
    total = functools.reduce(jnp.add, weights)
    safe = jnp.where(total > 0.0, total, 1.0)
    return [w / safe for w in weights], jnp.where(total > 0.0, top + jnp.log(safe), NEG)


def stacked(parts):
    return jnp.concatenate(parts, axis=0)


def head_cols(head, start=0):
    return slice(start + head * HD, start + (head + 1) * HD)


def put_pair(out_ref, start, out, lse):
    middle = start + QROWS
    out_ref[:, start:middle] = out.astype(bf16).reshape(KVH, QROWS, HD)
    for head in range(KVH):
        out_ref[head, middle : middle + STAT] = packed_stat(
            lse[head * QROWS : (head + 1) * QROWS]
        )


def front_kernel(
    owner_hbm,
    len_hbm,
    q_hbm,
    cache_hbm,
    acts_hbm,
    w_hbm,
    away_ref,
    value_ref,
    mine_ref,
    owner_ref,
    len_ref,
    q_ref,
    cache_ref,
    acts_ref,
    w_ref,
    sems,
):
    core = lax.axis_index("core")
    me = lax.axis_index("yx") * 2 + core
    slab = cache_ref.shape[1]
    span = acts_ref.shape[0]
    half = span // 2
    order = (1 - core, core)
    ints = [
        pltpu.make_async_copy(owner_hbm, owner_ref, sems.at[0]),
        pltpu.make_async_copy(len_hbm, len_ref, sems.at[1]),
        pltpu.make_async_copy(q_hbm, q_ref, sems.at[2]),
    ]
    loads = [
        pltpu.make_async_copy(cache_hbm.at[row], cache_ref.at[k], sems.at[3 + k])
        for k, row in enumerate(order)
    ]
    late = [
        pltpu.make_async_copy(acts_hbm, acts_ref, sems.at[5]),
        pltpu.make_async_copy(w_hbm.at[:, COLS : 2 * COLS], w_ref, sems.at[6]),
    ]
    for copy in (*ints, *loads, *late):
        copy.start()
    for copy in ints:
        copy.wait()
    for k, row in enumerate(order):
        first = jnp.int32(0)
        for block in range(owner_ref.shape[1]):
            first = first + jnp.where(owner_ref[row, block] == me, block, 0)
        room = len_ref[0, row] - first * slab
        live = lax.broadcasted_iota(jnp.int32, (KVH * QROWS, slab), 1) < room
        loads[k].wait()
        score = stacked(
            [dot_nt(q_ref[row, head], cache_ref[k, :, head_cols(head)]) for head in range(KVH)]
        )
        score = jnp.where(live, score * SCALE, NEG)
        top = jnp.max(score, axis=-1, keepdims=True)
        weight = jnp.where(live, jnp.exp(score - top), 0.0)
        total = jnp.sum(weight, axis=-1, keepdims=True)
        safe = jnp.where(total > 0.0, total, 1.0)
        weight = weight.astype(bf16)
        out = stacked(
            [
                dot_nn(
                    weight[head * QROWS : (head + 1) * QROWS],
                    cache_ref[k, :, head_cols(head, COLS)],
                )
                for head in range(KVH)
            ]
        )
        lse = jnp.where(total > 0.0, top + jnp.log(safe), NEG)
        if k == 0:
            put_pair(away_ref, half, out / safe, lse)
        else:
            put_pair(mine_ref, 0, out / safe, lse)
    for copy in late:
        copy.wait()
    for row, out_ref in zip(order, (away_ref, value_ref)):
        tokens = acts_ref[pl.ds(pl.multiple_of(row * half, half), half), :]
        value = dot_nn(tokens, w_ref[...]).astype(bf16)
        for head in range(KVH):
            out_ref[head, :half] = value[:, head_cols(head)]


def score_kernel(
    q_ref, acts_hbm, w_hbm, _, away_hbm, own_ref, acts_ref, w_ref, qw_ref, words_ref, sems
):
    core = lax.axis_index("core")
    half = acts_ref.shape[0] // 2
    loads = [
        pltpu.make_async_copy(w_hbm.at[:, 0:COLS], w_ref, sems.at[0]),
        pltpu.make_async_copy(acts_hbm, acts_ref, sems.at[1]),
    ]
    for copy in loads:
        copy.start()
    loads[0].wait()
    for head in range(KVH):
        rows = slice(head * QROWS, (head + 1) * QROWS)
        qw_ref[rows] = dot_nt(q_ref[head], w_ref[:, head_cols(head)]).astype(bf16)
    loads[1].wait()
    tiles = half // HD

    def tokens(row):
        return acts_ref[pl.ds(pl.multiple_of(row * half, half), half), :]

    score = dot_nt(qw_ref[...], tokens(1 - core)) * SCALE
    high = score.astype(bf16)
    low = (score - high.astype(f32)).astype(bf16)
    for part, words in enumerate((high, low)):
        for tile in range(tiles):
            at = (part * tiles + tile) * QROWS
            words_ref[:, at : at + QROWS] = words[:, head_cols(tile)].reshape(KVH, QROWS, HD)
    start = half + PAIR
    store = pltpu.make_async_copy(
        words_ref, away_hbm.at[:, start : start + 2 * tiles * QROWS], sems.at[2]
    )
    store.start()
    own_ref[...] = dot_nt(qw_ref[...], tokens(core)) * SCALE
    store.wait()


def pack_kernel(got_ref, value_ref, own_ref, mine_ref, out_ref):
    half = value_ref.shape[1]
    tiles = half // HD
    out_ref[:, :half] = (value_ref[...].astype(f32) + got_ref[:, :half].astype(f32)).astype(bf16)
    shape = (KVH, QROWS, HD)
    start = half + PAIR
    for tile in range(tiles):
        score = own_ref[:, head_cols(tile)].reshape(shape)
        for part in range(2):
            at = start + (part * tiles + tile) * QROWS
            score = score + got_ref[:, at : at + QROWS].astype(f32)
        at = half + tile * QROWS
        out_ref[:, at : at + QROWS] = score.astype(bf16)
    at = half + tiles * QROWS
    middle = at + QROWS
    pair = [
        [stat_row(ref[head, first : first + STAT]) for head in range(KVH)]
        for ref, first in ((mine_ref, QROWS), (got_ref, half + QROWS))
    ]
    weights, lse = shares([stacked(rows) for rows in pair])
    weights = columns(stacked(weights))
    packed = [jnp.concatenate(terms(lse[head : head + 1]), axis=0) for head in range(KVH)]
    for head in range(KVH):
        out_ref[head, at:middle] = (
            weights[head] * mine_ref[head, :QROWS].astype(f32)
            + weights[KVH + head] * got_ref[head, half : half + QROWS].astype(f32)
        ).astype(bf16)
        out_ref[head, middle : middle + STAT] = jnp.concatenate(
            [packed[head], jnp.zeros((STAT - 3, HD), f32)], axis=0
        ).astype(bf16)


def span_kernel(got_ref, q_ref, draft_ref, out_ref):
    parts, length, _ = got_ref.shape
    half = (length - PAIR) * HD // (HD + QROWS)
    tiles = half // HD
    role = lax.axis_index("role")
    core = lax.axis_index("core")
    head = lax.axis_index("yx")

    def total(start, size):
        acc = got_ref[0, start : start + size].astype(f32)
        for part in range(1, parts):
            acc = acc + got_ref[part, start : start + size].astype(f32)
        return acc

    value = total(0, half).astype(bf16)
    score = jnp.concatenate(
        [total(half + tile * QROWS, QROWS) for tile in range(tiles)], axis=1
    )
    out, lse = attend(score, value)
    fresh = stacked([out.astype(bf16), packed_stat(lse)])

    query = q_ref[core, head]
    start = pl.multiple_of(head * HD, HD)
    draft_keys = draft_ref[core, :, pl.ds(start, HD)].astype(f32)
    draft_vals = draft_ref[core, :, pl.ds(start + COLS, HD)].astype(f32)
    token = lax.broadcasted_iota(jnp.int32, (QROWS, 1), 0) % DRAFT
    scores = []
    for u in range(DRAFT):
        one = jnp.sum(query.astype(f32) * draft_keys[u : u + 1], axis=-1, keepdims=True) * SCALE
        scores.append(jnp.where(token >= u, one, NEG))
    top = functools.reduce(jnp.maximum, scores)
    weights = [jnp.where(one > 0.5 * NEG, jnp.exp(one - top), 0.0) for one in scores]
    sums = functools.reduce(jnp.add, weights)
    drafted = functools.reduce(
        jnp.add,
        [w.astype(bf16).astype(f32) * draft_vals[u : u + 1] for u, w in enumerate(weights)],
    )
    at = half + tiles * QROWS
    middle = at + QROWS
    rows = [stat_row(got_ref[part, middle : middle + STAT]) for part in range(parts)]
    rows.append(stat_row(packed_stat(top + jnp.log(sums))))
    weights, lse = shares(rows)
    weights = columns(stacked(weights))
    out = weights[parts] * (drafted / sums)
    for part in range(parts):
        out = out + weights[part] * got_ref[part, at:middle].astype(f32)
    spare = jnp.zeros((STAT - 3, HD), f32)
    kept = stacked([out.astype(bf16), stacked([*terms(lse), spare]).astype(bf16)])

    chunks = out_ref.shape[1]
    for chunk in range(chunks):
        out_ref[role, chunk] = kept
        out_ref[1 - role, chunk] = fresh


def join_kernel(span_ref, got_ref, out_ref):
    role = lax.axis_index("role")
    rows = out_ref.shape[0]

    def stats(pool, core):
        return stacked([stat_row(got_ref[pool, 2 * head + core, QROWS:]) for head in range(KVH)])

    fresh = [stats(1 - role, core) for core in range(2)]
    weights = []
    for row in range(rows):
        taken = span_ref[0, 0] == row
        kept = [jnp.where(taken, lse, NEG) for lse in fresh]
        weights += shares([stats(role, row), *kept])[0]
    weights = columns(stacked(weights))
    for row in range(rows):
        for head in range(KVH):
            sources = [(role, row), (1 - role, 0), (1 - role, 1)]
            out = jnp.zeros((QROWS, HD), f32)
            for k, (pool, core) in enumerate(sources):
                weight = weights[(row * 3 + k) * KVH + head]
                out = out + weight * got_ref[pool, 2 * head + core, :QROWS].astype(f32)
            out_ref[row, head] = out.astype(bf16)


def call(kernel, out_shapes, spaces, scratch=(), flops=0, moved=0, limit=24, aliases=None):
    out_specs = jax.tree.map(lambda _: pl.BlockSpec(memory_space=pltpu.VMEM), out_shapes)
    for target in (aliases or {}).values():
        out_specs[target] = pl.BlockSpec(memory_space=H)
    return pl.pallas_call(
        kernel,
        out_shape=out_shapes,
        in_specs=[pl.BlockSpec(memory_space=space) for space in spaces],
        out_specs=out_specs,
        input_output_aliases=aliases or {},
        scratch_shapes=list(scratch),
        compiler_params=pltpu.CompilerParams(vmem_limit_bytes=limit << 20),
        cost_estimate=pl.CostEstimate(flops=flops, bytes_accessed=moved, transcendentals=0),
    )


V = pltpu.VMEM
S = pltpu.SMEM
H = pltpu.HBM
FRONT = 58
SCORE = 52


def shards(
    prompt_acts, kv_weight, cache_kv, cache_len, block_owner, span_row, draft_query, draft_kv
):
    swap = [(0, 1), (1, 0)]
    acts = prompt_acts[0, 0]
    span, width = acts.shape
    half = span // 2
    rows = cache_kv.shape[1]
    n_yx = lax.axis_size("yx")
    struct = jax.ShapeDtypeStruct

    query = draft_query[0].reshape(rows, DRAFT, KVH, GROUP, HD).transpose(0, 2, 3, 1, 4)
    query = query.reshape(rows, KVH, QROWS, HD)
    chosen = query[0]
    for row in range(1, rows):
        chosen = jnp.where(span_row[0] == row, query[row], chosen)
    asked = lax.ppermute(chosen, "role", swap)

    dma = pltpu.SemaphoreType.DMA
    words = 2 * (half // HD) * QROWS
    away = struct((KVH, half + PAIR + words, HD), bf16)
    away, value, mine = call(
        front_kernel,
        [away, struct((KVH, half, HD), bf16), struct((KVH, PAIR, HD), bf16)],
        [H] * 6,
        [
            S(block_owner.shape[1:], jnp.int32),
            S(cache_len.shape, jnp.int32),
            V(query.shape, bf16),
            V(cache_kv.shape[1:], bf16),
            V(acts.shape, bf16),
            V((width, COLS), bf16),
            dma((7,)),
        ],
        flops=1_500_000_000,
        moved=6_000_000,
        limit=FRONT,
    )(block_owner[0], cache_len, query, cache_kv[0], acts, kv_weight)
    asked, away = lax.optimization_barrier((asked, away))
    away, own = call(
        score_kernel,
        [struct(away.shape, bf16), struct((KVH * QROWS, half), f32)],
        [V, H, H, H],
        [
            V(acts.shape, bf16),
            V((width, COLS), bf16),
            V((KVH * QROWS, width), bf16),
            V((KVH, words, HD), bf16),
            dma((3,)),
        ],
        flops=600_000_000,
        moved=3_000_000,
        limit=SCORE,
        aliases={3: 0},
    )(asked, acts, kv_weight, away)
    theirs = lax.ppermute(away, "core", swap)
    sent = call(
        pack_kernel,
        struct((KVH, half + (half // HD) * QROWS + PAIR, HD), bf16),
        [V] * 4,
        flops=10_000_000,
        moved=5_000_000,
    )(theirs, value, own, mine)
    got = lax.all_to_all(sent, "yx", 0, 0, tiled=True)

    parts = call(
        span_kernel,
        struct((2, 2 * n_yx, PAIR, HD), bf16),
        [V, V, V],
        flops=20_000_000,
        moved=3_000_000,
    )(got, query, draft_kv[0])
    parts = lax.all_to_all(
        parts.reshape(4 * n_yx, PAIR, HD), ("role", "yx", "core"), 0, 0, tiled=True
    )
    joined = call(
        join_kernel, struct((rows, KVH, QROWS, HD), bf16), [S, V], flops=10_000_000, moved=700_000
    )(span_row, parts.reshape(2, 2 * n_yx, PAIR, HD))
    output = joined.reshape(rows, KVH, GROUP, DRAFT, HD).transpose(0, 3, 1, 2, 4)
    return output.reshape(1, rows, DRAFT, QH * HD)


def solution(mesh):
    roles, groups, tps = mesh.devices.shape
    fine = Mesh(mesh.devices.reshape(roles, groups, tps // 2, 2), ("role", "grp", "yx", "core"))
    tp = ("yx", "core")
    placed = (
        P("role", "grp", None, tp),
        P(tp, None),
        P("role", "grp", tp, None),
        P("role", "grp"),
        P("role", "grp", None),
        P("role", "grp"),
        P("role", "grp", None, None),
        P("role", "grp", None, None),
    )
    return jax.shard_map(
        shards, mesh=fine, in_specs=placed, out_specs=P("role", "grp", None, None), check_vma=False
    )
```

```python
import functools
import math

import jax
import jax.numpy as jnp
from jax import lax
from jax.experimental import pallas as pl
from jax.experimental.pallas import tpu as pltpu
from jax.sharding import Mesh
from jax.sharding import PartitionSpec as P

QH = 64
KVH = 8
HD = 128
DRAFT = 4
GROUP = QH // KVH
QROWS = GROUP * DRAFT
STAT = 16
PAIR = QROWS + STAT
COLS = KVH * HD
NEG = -1e30
SCALE = 1.0 / math.sqrt(HD)

f32 = jnp.float32
bf16 = jnp.bfloat16


def dot_nt(a, b):
    return lax.dot_general(a, b, (((1,), (1,)), ((), ())), preferred_element_type=f32)


def dot_nn(a, b):
    return jnp.dot(a, b, preferred_element_type=f32)


def terms(lse):
    hi = lse.astype(bf16).astype(f32)
    mid = (lse - hi).astype(bf16).astype(f32)
    return hi, mid, lse - hi - mid


def packed_stat(lse):
    lane = lax.broadcasted_iota(jnp.int32, (QROWS, HD), 1)
    tile = jnp.zeros((QROWS, HD), f32)
    for at, term in enumerate(terms(lse)):
        tile = jnp.where(lane == at, term, tile)
    rows = tile.T[:STAT]
    return jnp.concatenate([rows, jnp.zeros((STAT, HD - QROWS), f32)], axis=1).astype(bf16)


def stat_row(tile):
    rows = tile.astype(f32)
    return rows[0:1] + rows[1:2] + rows[2:3]


def columns(rows):
    count = rows.shape[0]
    square = jnp.concatenate([rows, jnp.zeros((HD - count, HD), f32)], axis=0).T
    return [square[:QROWS, k : k + 1] for k in range(count)]


def attend(score, value):
    top = jnp.max(score, axis=-1, keepdims=True)
    weight = jnp.where(score > 0.5 * NEG, jnp.exp(score - top), 0.0)
    total = jnp.sum(weight, axis=-1, keepdims=True)
    any_key = total > 0.0
    safe = jnp.where(any_key, total, 1.0)
    out = dot_nn(weight.astype(bf16), value) / safe
    return out, jnp.where(any_key, top + jnp.log(safe), NEG)


def shares(rows):
    top = functools.reduce(jnp.maximum, rows)
    weights = [jnp.where(row > 0.5 * NEG, jnp.exp(row - top), 0.0) for row in rows]
    total = functools.reduce(jnp.add, weights)
    safe = jnp.where(total > 0.0, total, 1.0)
    return [w / safe for w in weights], jnp.where(total > 0.0, top + jnp.log(safe), NEG)


def stacked(parts):
    return jnp.concatenate(parts, axis=0)


def head_cols(head, start=0):
    return slice(start + head * HD, start + (head + 1) * HD)


def put_pair(out_ref, start, out, lse):
    middle = start + QROWS
    out_ref[:, start:middle] = out.astype(bf16).reshape(KVH, QROWS, HD)
    for head in range(KVH):
        out_ref[head, middle : middle + STAT] = packed_stat(
            lse[head * QROWS : (head + 1) * QROWS]
        )


def front_kernel(
    owner_hbm,
    len_hbm,
    q_hbm,
    cache_hbm,
    acts_hbm,
    w_hbm,
    away_ref,
    value_ref,
    mine_ref,
    owner_ref,
    len_ref,
    q_ref,
    cache_ref,
    acts_ref,
    w_ref,
    sems,
):
    core = lax.axis_index("core")
    me = lax.axis_index("yx") * 2 + core
    slab = cache_ref.shape[1]
    span = acts_ref.shape[0]
    half = span // 2
    order = (1 - core, core)
    ints = [
        pltpu.make_async_copy(owner_hbm, owner_ref, sems.at[0]),
        pltpu.make_async_copy(len_hbm, len_ref, sems.at[1]),
        pltpu.make_async_copy(q_hbm, q_ref, sems.at[2]),
    ]
    loads = [
        pltpu.make_async_copy(cache_hbm.at[row], cache_ref.at[k], sems.at[3 + k])
        for k, row in enumerate(order)
    ]
    late = [
        pltpu.make_async_copy(acts_hbm, acts_ref, sems.at[5]),
        pltpu.make_async_copy(w_hbm.at[:, COLS : 2 * COLS], w_ref, sems.at[6]),
    ]
    for copy in (*ints, *loads, *late):
        copy.start()
    for copy in ints:
        copy.wait()
    for k, row in enumerate(order):
        first = jnp.int32(0)
        for block in range(owner_ref.shape[1]):
            first = first + jnp.where(owner_ref[row, block] == me, block, 0)
        room = len_ref[0, row] - first * slab
        live = lax.broadcasted_iota(jnp.int32, (KVH * QROWS, slab), 1) < room
        loads[k].wait()
        score = stacked(
            [dot_nt(q_ref[row, head], cache_ref[k, :, head_cols(head)]) for head in range(KVH)]
        )
        score = jnp.where(live, score * SCALE, NEG)
        top = jnp.max(score, axis=-1, keepdims=True)
        weight = jnp.where(live, jnp.exp(score - top), 0.0)
        total = jnp.sum(weight, axis=-1, keepdims=True)
        safe = jnp.where(total > 0.0, total, 1.0)
        weight = weight.astype(bf16)
        out = stacked(
            [
                dot_nn(
                    weight[head * QROWS : (head + 1) * QROWS],
                    cache_ref[k, :, head_cols(head, COLS)],
                )
                for head in range(KVH)
            ]
        )
        lse = jnp.where(total > 0.0, top + jnp.log(safe), NEG)
        if k == 0:
            put_pair(away_ref, half, out / safe, lse)
        else:
            put_pair(mine_ref, 0, out / safe, lse)
    for copy in late:
        copy.wait()
    for row, out_ref in zip(order, (away_ref, value_ref)):
        tokens = acts_ref[pl.ds(pl.multiple_of(row * half, half), half), :]
        value = dot_nn(tokens, w_ref[...]).astype(bf16)
        for head in range(KVH):
            out_ref[head, :half] = value[:, head_cols(head)]


def score_kernel(q_ref, acts_ref, w_hbm, _, away_hbm, qw_ref, w_ref, words_ref, sems):
    core = lax.axis_index("core")
    half = acts_ref.shape[0] // 2
    middle = COLS // 2
    loads = [
        pltpu.make_async_copy(w_hbm.at[:, cols], w_ref.at[:, cols], sems.at[k])
        for k, cols in enumerate((slice(0, middle), slice(middle, COLS)))
    ]
    for copy in loads:
        copy.start()
    for head in range(KVH):
        if head * HD % middle == 0:
            loads[head * HD // middle].wait()
        rows = slice(head * QROWS, (head + 1) * QROWS)
        qw_ref[rows] = dot_nt(q_ref[head], w_ref[:, head_cols(head)]).astype(bf16)
    start = pl.multiple_of((1 - core) * half, half)
    score = (dot_nt(qw_ref[...], acts_ref[pl.ds(start, half), :]) * SCALE).astype(bf16)
    tiles = half // HD
    for tile in range(tiles):
        at = tile * QROWS
        words_ref[:, at : at + QROWS] = score[:, head_cols(tile)].reshape(KVH, QROWS, HD)
    store = pltpu.make_async_copy(
        words_ref, away_hbm.at[:, half + PAIR : half + PAIR + tiles * QROWS], sems.at[2]
    )
    store.start()
    store.wait()


def own_kernel(qw_ref, acts_ref, own_ref):
    half = acts_ref.shape[0] // 2
    start = pl.multiple_of(lax.axis_index("core") * half, half)
    own_ref[...] = dot_nt(qw_ref[...], acts_ref[pl.ds(start, half), :]) * SCALE


def pack_kernel(got_ref, value_ref, own_ref, mine_ref, out_ref):
    half = value_ref.shape[1]
    tiles = half // HD
    out_ref[:, :half] = (value_ref[...].astype(f32) + got_ref[:, :half].astype(f32)).astype(bf16)
    shape = (KVH, QROWS, HD)
    start = half + PAIR
    for tile in range(tiles):
        score = own_ref[:, head_cols(tile)].reshape(shape)
        at = start + tile * QROWS
        score = score + got_ref[:, at : at + QROWS].astype(f32)
        at = half + tile * QROWS
        out_ref[:, at : at + QROWS] = score.astype(bf16)
    at = half + tiles * QROWS
    middle = at + QROWS
    pair = [
        [stat_row(ref[head, first : first + STAT]) for head in range(KVH)]
        for ref, first in ((mine_ref, QROWS), (got_ref, half + QROWS))
    ]
    weights, lse = shares([stacked(rows) for rows in pair])
    weights = columns(stacked(weights))
    packed = [jnp.concatenate(terms(lse[head : head + 1]), axis=0) for head in range(KVH)]
    for head in range(KVH):
        out_ref[head, at:middle] = (
            weights[head] * mine_ref[head, :QROWS].astype(f32)
            + weights[KVH + head] * got_ref[head, half : half + QROWS].astype(f32)
        ).astype(bf16)
        out_ref[head, middle : middle + STAT] = jnp.concatenate(
            [packed[head], jnp.zeros((STAT - 3, HD), f32)], axis=0
        ).astype(bf16)


def span_kernel(got_ref, q_ref, draft_ref, out_ref):
    parts, length, _ = got_ref.shape
    half = (length - PAIR) * HD // (HD + QROWS)
    tiles = half // HD
    role = lax.axis_index("role")
    core = lax.axis_index("core")
    head = lax.axis_index("yx")

    def total(start, size):
        acc = got_ref[0, start : start + size].astype(f32)
        for part in range(1, parts):
            acc = acc + got_ref[part, start : start + size].astype(f32)
        return acc

    value = total(0, half).astype(bf16)
    score = jnp.concatenate(
        [total(half + tile * QROWS, QROWS) for tile in range(tiles)], axis=1
    )
    out, lse = attend(score, value)
    fresh = stacked([out.astype(bf16), packed_stat(lse)])

    query = q_ref[core, head]
    start = pl.multiple_of(head * HD, HD)
    draft_keys = draft_ref[core, :, pl.ds(start, HD)].astype(f32)
    draft_vals = draft_ref[core, :, pl.ds(start + COLS, HD)].astype(f32)
    token = lax.broadcasted_iota(jnp.int32, (QROWS, 1), 0) % DRAFT
    scores = []
    for u in range(DRAFT):
        one = jnp.sum(query.astype(f32) * draft_keys[u : u + 1], axis=-1, keepdims=True) * SCALE
        scores.append(jnp.where(token >= u, one, NEG))
    top = functools.reduce(jnp.maximum, scores)
    weights = [jnp.where(one > 0.5 * NEG, jnp.exp(one - top), 0.0) for one in scores]
    sums = functools.reduce(jnp.add, weights)
    drafted = functools.reduce(
        jnp.add,
        [w.astype(bf16).astype(f32) * draft_vals[u : u + 1] for u, w in enumerate(weights)],
    )
    at = half + tiles * QROWS
    middle = at + QROWS
    rows = [stat_row(got_ref[part, middle : middle + STAT]) for part in range(parts)]
    rows.append(stat_row(packed_stat(top + jnp.log(sums))))
    weights, lse = shares(rows)
    weights = columns(stacked(weights))
    out = weights[parts] * (drafted / sums)
    for part in range(parts):
        out = out + weights[part] * got_ref[part, at:middle].astype(f32)
    spare = jnp.zeros((STAT - 3, HD), f32)
    kept = stacked([out.astype(bf16), stacked([*terms(lse), spare]).astype(bf16)])

    chunks = out_ref.shape[1]
    for chunk in range(chunks):
        out_ref[role, chunk] = kept
        out_ref[1 - role, chunk] = fresh


def join_kernel(span_ref, got_ref, out_ref):
    role = lax.axis_index("role")
    rows = out_ref.shape[0]

    def stats(pool, core):
        return stacked([stat_row(got_ref[pool, 2 * head + core, QROWS:]) for head in range(KVH)])

    fresh = [stats(1 - role, core) for core in range(2)]
    weights = []
    for row in range(rows):
        taken = span_ref[0, 0] == row
        kept = [jnp.where(taken, lse, NEG) for lse in fresh]
        weights += shares([stats(role, row), *kept])[0]
    weights = columns(stacked(weights))
    for row in range(rows):
        for head in range(KVH):
            sources = [(role, row), (1 - role, 0), (1 - role, 1)]
            out = jnp.zeros((QROWS, HD), f32)
            for k, (pool, core) in enumerate(sources):
                weight = weights[(row * 3 + k) * KVH + head]
                out = out + weight * got_ref[pool, 2 * head + core, :QROWS].astype(f32)
            out_ref[row, head] = out.astype(bf16)


def call(kernel, out_shapes, spaces, scratch=(), flops=0, moved=0, limit=24, aliases=None):
    out_specs = jax.tree.map(lambda _: pl.BlockSpec(memory_space=pltpu.VMEM), out_shapes)
    for target in (aliases or {}).values():
        out_specs[target] = pl.BlockSpec(memory_space=H)
    return pl.pallas_call(
        kernel,
        out_shape=out_shapes,
        in_specs=[pl.BlockSpec(memory_space=space) for space in spaces],
        out_specs=out_specs,
        input_output_aliases=aliases or {},
        scratch_shapes=list(scratch),
        compiler_params=pltpu.CompilerParams(vmem_limit_bytes=limit << 20),
        cost_estimate=pl.CostEstimate(flops=flops, bytes_accessed=moved, transcendentals=0),
    )


V = pltpu.VMEM
S = pltpu.SMEM
H = pltpu.HBM
FRONT = 58
SCORE = 52


def shards(
    prompt_acts, kv_weight, cache_kv, cache_len, block_owner, span_row, draft_query, draft_kv
):
    swap = [(0, 1), (1, 0)]
    acts = prompt_acts[0, 0]
    span, width = acts.shape
    half = span // 2
    rows = cache_kv.shape[1]
    n_yx = lax.axis_size("yx")
    struct = jax.ShapeDtypeStruct

    query = draft_query[0].reshape(rows, DRAFT, KVH, GROUP, HD).transpose(0, 2, 3, 1, 4)
    query = query.reshape(rows, KVH, QROWS, HD)
    chosen = query[0]
    for row in range(1, rows):
        chosen = jnp.where(span_row[0] == row, query[row], chosen)
    asked = lax.ppermute(chosen, "role", swap)

    dma = pltpu.SemaphoreType.DMA
    words = (half // HD) * QROWS
    away = struct((KVH, half + PAIR + words, HD), bf16)
    away, value, mine = call(
        front_kernel,
        [away, struct((KVH, half, HD), bf16), struct((KVH, PAIR, HD), bf16)],
        [H] * 6,
        [
            S(block_owner.shape[1:], jnp.int32),
            S(cache_len.shape, jnp.int32),
            V(query.shape, bf16),
            V(cache_kv.shape[1:], bf16),
            V(acts.shape, bf16),
            V((width, COLS), bf16),
            dma((7,)),
        ],
        flops=1_500_000_000,
        moved=6_000_000,
        limit=FRONT,
    )(block_owner[0], cache_len, query, cache_kv[0], acts, kv_weight)
    asked, away = lax.optimization_barrier((asked, away))
    away, absorbed = call(
        score_kernel,
        [struct(away.shape, bf16), struct((KVH * QROWS, width), bf16)],
        [V, V, H, H],
        [V((width, COLS), bf16), V((KVH, words, HD), bf16), dma((3,))],
        flops=300_000_000,
        moved=3_000_000,
        limit=SCORE,
        aliases={3: 0},
    )(asked, acts, kv_weight, away)
    theirs = lax.ppermute(away, "core", swap)
    own = call(
        own_kernel,
        struct((KVH * QROWS, half), f32),
        [V, V],
        flops=140_000_000,
        moved=2_000_000,
    )(absorbed, acts)
    sent = call(
        pack_kernel,
        struct((KVH, half + (half // HD) * QROWS + PAIR, HD), bf16),
        [V] * 4,
        flops=10_000_000,
        moved=5_000_000,
    )(theirs, value, own, mine)
    got = lax.all_to_all(sent, "yx", 0, 0, tiled=True)

    parts = call(
        span_kernel,
        struct((2, 2 * n_yx, PAIR, HD), bf16),
        [V, V, V],
        flops=20_000_000,
        moved=3_000_000,
    )(got, query, draft_kv[0])
    parts = lax.all_to_all(
        parts.reshape(4 * n_yx, PAIR, HD), ("role", "yx", "core"), 0, 0, tiled=True
    )
    joined = call(
        join_kernel, struct((rows, KVH, QROWS, HD), bf16), [S, V], flops=10_000_000, moved=700_000
    )(span_row, parts.reshape(2, 2 * n_yx, PAIR, HD))
    output = joined.reshape(rows, KVH, GROUP, DRAFT, HD).transpose(0, 3, 1, 2, 4)
    return output.reshape(1, rows, DRAFT, QH * HD)


def solution(mesh):
    roles, groups, tps = mesh.devices.shape
    fine = Mesh(mesh.devices.reshape(roles, groups, tps // 2, 2), ("role", "grp", "yx", "core"))
    tp = ("yx", "core")
    placed = (
        P("role", "grp", None, tp),
        P(tp, None),
        P("role", "grp", tp, None),
        P("role", "grp"),
        P("role", "grp", None),
        P("role", "grp"),
        P("role", "grp", None, None),
        P("role", "grp", None, None),
    )
    return jax.shard_map(
        shards, mesh=fine, in_specs=placed, out_specs=P("role", "grp", None, None), check_vma=False
    )
```

```python
import functools
import math

import jax
import jax.numpy as jnp
from jax import lax
from jax.experimental import pallas as pl
from jax.experimental.pallas import tpu as pltpu
from jax.sharding import Mesh
from jax.sharding import PartitionSpec as P

QH = 64
KVH = 8
HD = 128
DRAFT = 4
GROUP = QH // KVH
QROWS = GROUP * DRAFT
STAT = 16
PAIR = QROWS + STAT
COLS = KVH * HD
NEG = -1e30
SCALE = 1.0 / math.sqrt(HD)

f32 = jnp.float32
bf16 = jnp.bfloat16


def dot_nt(a, b):
    return lax.dot_general(a, b, (((1,), (1,)), ((), ())), preferred_element_type=f32)


def dot_nn(a, b):
    return jnp.dot(a, b, preferred_element_type=f32)


def terms(lse):
    hi = lse.astype(bf16).astype(f32)
    mid = (lse - hi).astype(bf16).astype(f32)
    return hi, mid, lse - hi - mid


def packed_stat(lse):
    lane = lax.broadcasted_iota(jnp.int32, (QROWS, HD), 1)
    tile = jnp.zeros((QROWS, HD), f32)
    for at, term in enumerate(terms(lse)):
        tile = jnp.where(lane == at, term, tile)
    rows = tile.T[:STAT]
    return jnp.concatenate([rows, jnp.zeros((STAT, HD - QROWS), f32)], axis=1).astype(bf16)


def stat_row(tile):
    rows = tile.astype(f32)
    return rows[0:1] + rows[1:2] + rows[2:3]


def columns(rows):
    count = rows.shape[0]
    square = jnp.concatenate([rows, jnp.zeros((HD - count, HD), f32)], axis=0).T
    return [square[:QROWS, k : k + 1] for k in range(count)]


def attend(score, value):
    top = jnp.max(score, axis=-1, keepdims=True)
    weight = jnp.where(score > 0.5 * NEG, jnp.exp(score - top), 0.0)
    total = jnp.sum(weight, axis=-1, keepdims=True)
    any_key = total > 0.0
    safe = jnp.where(any_key, total, 1.0)
    out = dot_nn(weight.astype(bf16), value) / safe
    return out, jnp.where(any_key, top + jnp.log(safe), NEG)


def shares(rows):
    top = functools.reduce(jnp.maximum, rows)
    weights = [jnp.where(row > 0.5 * NEG, jnp.exp(row - top), 0.0) for row in rows]
    total = functools.reduce(jnp.add, weights)
    safe = jnp.where(total > 0.0, total, 1.0)
    return [w / safe for w in weights], jnp.where(total > 0.0, top + jnp.log(safe), NEG)


def stacked(parts):
    return jnp.concatenate(parts, axis=0)


def head_cols(head, start=0):
    return slice(start + head * HD, start + (head + 1) * HD)


def put_pair(out_ref, start, out, lse):
    middle = start + QROWS
    out_ref[:, start:middle] = out.astype(bf16).reshape(KVH, QROWS, HD)
    for head in range(KVH):
        out_ref[head, middle : middle + STAT] = packed_stat(
            lse[head * QROWS : (head + 1) * QROWS]
        )


def front_kernel(
    owner_hbm,
    len_hbm,
    q_hbm,
    cache_hbm,
    acts_hbm,
    w_hbm,
    away_ref,
    value_ref,
    mine_ref,
    owner_ref,
    len_ref,
    q_ref,
    cache_ref,
    acts_ref,
    w_ref,
    sems,
):
    core = lax.axis_index("core")
    me = lax.axis_index("yx") * 2 + core
    slab = cache_ref.shape[1]
    span = acts_ref.shape[0]
    half = span // 2
    order = (1 - core, core)
    ints = [
        pltpu.make_async_copy(owner_hbm, owner_ref, sems.at[0]),
        pltpu.make_async_copy(len_hbm, len_ref, sems.at[1]),
        pltpu.make_async_copy(q_hbm, q_ref, sems.at[2]),
    ]
    loads = [
        pltpu.make_async_copy(cache_hbm.at[row], cache_ref.at[k], sems.at[3 + k])
        for k, row in enumerate(order)
    ]
    late = [
        pltpu.make_async_copy(acts_hbm, acts_ref, sems.at[5]),
        pltpu.make_async_copy(w_hbm.at[:, COLS : 2 * COLS], w_ref, sems.at[6]),
    ]
    for copy in (*ints, *loads, *late):
        copy.start()
    for copy in ints:
        copy.wait()
    for k, row in enumerate(order):
        first = jnp.int32(0)
        for block in range(owner_ref.shape[1]):
            first = first + jnp.where(owner_ref[row, block] == me, block, 0)
        room = len_ref[0, row] - first * slab
        live = lax.broadcasted_iota(jnp.int32, (KVH * QROWS, slab), 1) < room
        loads[k].wait()
        score = stacked(
            [dot_nt(q_ref[row, head], cache_ref[k, :, head_cols(head)]) for head in range(KVH)]
        )
        score = jnp.where(live, score * SCALE, NEG)
        top = jnp.max(score, axis=-1, keepdims=True)
        weight = jnp.where(live, jnp.exp(score - top), 0.0)
        total = jnp.sum(weight, axis=-1, keepdims=True)
        safe = jnp.where(total > 0.0, total, 1.0)
        weight = weight.astype(bf16)
        out = stacked(
            [
                dot_nn(
                    weight[head * QROWS : (head + 1) * QROWS],
                    cache_ref[k, :, head_cols(head, COLS)],
                )
                for head in range(KVH)
            ]
        )
        lse = jnp.where(total > 0.0, top + jnp.log(safe), NEG)
        if k == 0:
            put_pair(away_ref, half, out / safe, lse)
        else:
            put_pair(mine_ref, 0, out / safe, lse)
    for copy in late:
        copy.wait()
    for row, out_ref in zip(order, (away_ref, value_ref)):
        tokens = acts_ref[pl.ds(pl.multiple_of(row * half, half), half), :]
        value = dot_nn(tokens, w_ref[...]).astype(bf16)
        for head in range(KVH):
            out_ref[head, :half] = value[:, head_cols(head)]


def absorb_kernel(span_ref, q_hbm, w_hbm, out_ref, q_ref, w_ref, sems):
    middle = COLS // 2
    row = span_ref[0, 0]
    first = pltpu.make_async_copy(q_hbm.at[row], q_ref, sems.at[2])
    loads = [
        pltpu.make_async_copy(w_hbm.at[:, cols], w_ref.at[:, cols], sems.at[k])
        for k, cols in enumerate((slice(0, middle), slice(middle, COLS)))
    ]
    for copy in (first, *loads):
        copy.start()
    first.wait()
    for head in range(KVH):
        if head * HD % middle == 0:
            loads[head * HD // middle].wait()
        rows = slice(head * QROWS, (head + 1) * QROWS)
        out_ref[rows] = dot_nt(q_ref[head], w_ref[:, head_cols(head)]).astype(bf16)


def other_kernel(qw_ref, acts_ref, out_ref):
    half = acts_ref.shape[0] // 2
    start = pl.multiple_of((1 - lax.axis_index("core")) * half, half)
    score = (dot_nt(qw_ref[...], acts_ref[pl.ds(start, half), :]) * SCALE).astype(bf16)
    for tile in range(half // HD):
        at = tile * QROWS
        out_ref[:, at : at + QROWS] = score[:, head_cols(tile)].reshape(KVH, QROWS, HD)


def own_kernel(qw_ref, acts_ref, own_ref):
    half = acts_ref.shape[0] // 2
    start = pl.multiple_of(lax.axis_index("core") * half, half)
    own_ref[...] = dot_nt(qw_ref[...], acts_ref[pl.ds(start, half), :]) * SCALE


def pack_kernel(got_ref, score_ref, value_ref, own_ref, mine_ref, out_ref):
    half = value_ref.shape[1]
    tiles = half // HD
    out_ref[:, :half] = (value_ref[...].astype(f32) + got_ref[:, :half].astype(f32)).astype(bf16)
    shape = (KVH, QROWS, HD)
    for tile in range(tiles):
        at = tile * QROWS
        score = own_ref[:, head_cols(tile)].reshape(shape)
        score = score + score_ref[:, at : at + QROWS].astype(f32)
        at = half + at
        out_ref[:, at : at + QROWS] = score.astype(bf16)
    at = half + tiles * QROWS
    middle = at + QROWS
    pair = [
        [stat_row(ref[head, first : first + STAT]) for head in range(KVH)]
        for ref, first in ((mine_ref, QROWS), (got_ref, half + QROWS))
    ]
    weights, lse = shares([stacked(rows) for rows in pair])
    weights = columns(stacked(weights))
    packed = [jnp.concatenate(terms(lse[head : head + 1]), axis=0) for head in range(KVH)]
    for head in range(KVH):
        out_ref[head, at:middle] = (
            weights[head] * mine_ref[head, :QROWS].astype(f32)
            + weights[KVH + head] * got_ref[head, half : half + QROWS].astype(f32)
        ).astype(bf16)
        out_ref[head, middle : middle + STAT] = jnp.concatenate(
            [packed[head], jnp.zeros((STAT - 3, HD), f32)], axis=0
        ).astype(bf16)


def span_kernel(got_ref, q_ref, draft_ref, out_ref):
    parts, length, _ = got_ref.shape
    half = (length - PAIR) * HD // (HD + QROWS)
    tiles = half // HD
    role = lax.axis_index("role")
    core = lax.axis_index("core")
    head = lax.axis_index("yx")

    def total(start, size):
        acc = got_ref[0, start : start + size].astype(f32)
        for part in range(1, parts):
            acc = acc + got_ref[part, start : start + size].astype(f32)
        return acc

    value = total(0, half).astype(bf16)
    score = jnp.concatenate(
        [total(half + tile * QROWS, QROWS) for tile in range(tiles)], axis=1
    )
    out, lse = attend(score, value)
    fresh = stacked([out.astype(bf16), packed_stat(lse)])

    query = q_ref[core, head]
    start = pl.multiple_of(head * HD, HD)
    draft_keys = draft_ref[core, :, pl.ds(start, HD)].astype(f32)
    draft_vals = draft_ref[core, :, pl.ds(start + COLS, HD)].astype(f32)
    token = lax.broadcasted_iota(jnp.int32, (QROWS, 1), 0) % DRAFT
    scores = []
    for u in range(DRAFT):
        one = jnp.sum(query.astype(f32) * draft_keys[u : u + 1], axis=-1, keepdims=True) * SCALE
        scores.append(jnp.where(token >= u, one, NEG))
    top = functools.reduce(jnp.maximum, scores)
    weights = [jnp.where(one > 0.5 * NEG, jnp.exp(one - top), 0.0) for one in scores]
    sums = functools.reduce(jnp.add, weights)
    drafted = functools.reduce(
        jnp.add,
        [w.astype(bf16).astype(f32) * draft_vals[u : u + 1] for u, w in enumerate(weights)],
    )
    at = half + tiles * QROWS
    middle = at + QROWS
    rows = [stat_row(got_ref[part, middle : middle + STAT]) for part in range(parts)]
    rows.append(stat_row(packed_stat(top + jnp.log(sums))))
    weights, lse = shares(rows)
    weights = columns(stacked(weights))
    out = weights[parts] * (drafted / sums)
    for part in range(parts):
        out = out + weights[part] * got_ref[part, at:middle].astype(f32)
    spare = jnp.zeros((STAT - 3, HD), f32)
    kept = stacked([out.astype(bf16), stacked([*terms(lse), spare]).astype(bf16)])

    chunks = out_ref.shape[1]
    for chunk in range(chunks):
        out_ref[role, chunk] = kept
        out_ref[1 - role, chunk] = fresh


def join_kernel(span_ref, got_ref, out_ref):
    role = lax.axis_index("role")
    rows = out_ref.shape[0]

    def stats(pool, core):
        return stacked([stat_row(got_ref[pool, 2 * head + core, QROWS:]) for head in range(KVH)])

    fresh = [stats(1 - role, core) for core in range(2)]
    weights = []
    for row in range(rows):
        taken = span_ref[0, 0] == row
        kept = [jnp.where(taken, lse, NEG) for lse in fresh]
        weights += shares([stats(role, row), *kept])[0]
    weights = columns(stacked(weights))
    for row in range(rows):
        for head in range(KVH):
            sources = [(role, row), (1 - role, 0), (1 - role, 1)]
            out = jnp.zeros((QROWS, HD), f32)
            for k, (pool, core) in enumerate(sources):
                weight = weights[(row * 3 + k) * KVH + head]
                out = out + weight * got_ref[pool, 2 * head + core, :QROWS].astype(f32)
            out_ref[row, head] = out.astype(bf16)


def call(kernel, out_shapes, spaces, scratch=(), flops=0, moved=0, limit=24, aliases=None):
    out_specs = jax.tree.map(lambda _: pl.BlockSpec(memory_space=pltpu.VMEM), out_shapes)
    for target in (aliases or {}).values():
        out_specs[target] = pl.BlockSpec(memory_space=H)
    return pl.pallas_call(
        kernel,
        out_shape=out_shapes,
        in_specs=[pl.BlockSpec(memory_space=space) for space in spaces],
        out_specs=out_specs,
        input_output_aliases=aliases or {},
        scratch_shapes=list(scratch),
        compiler_params=pltpu.CompilerParams(vmem_limit_bytes=limit << 20),
        cost_estimate=pl.CostEstimate(flops=flops, bytes_accessed=moved, transcendentals=0),
    )


V = pltpu.VMEM
S = pltpu.SMEM
H = pltpu.HBM
FRONT = 58


def shards(
    prompt_acts, kv_weight, cache_kv, cache_len, block_owner, span_row, draft_query, draft_kv
):
    swap = [(0, 1), (1, 0)]
    acts = prompt_acts[0, 0]
    span, width = acts.shape
    half = span // 2
    rows = cache_kv.shape[1]
    n_yx = lax.axis_size("yx")
    struct = jax.ShapeDtypeStruct

    query = draft_query[0].reshape(rows, DRAFT, KVH, GROUP, HD).transpose(0, 2, 3, 1, 4)
    query = query.reshape(rows, KVH, QROWS, HD)
    dma = pltpu.SemaphoreType.DMA
    absorbed = call(
        absorb_kernel,
        struct((KVH * QROWS, width), bf16),
        [S, H, H],
        [V(query.shape[1:], bf16), V((width, COLS), bf16), dma((3,))],
        flops=70_000_000,
        moved=1_500_000,
        limit=FRONT,
    )(span_row, query, kv_weight)
    asked = lax.ppermute(absorbed, "role", swap)
    absorbed, own_query = lax.optimization_barrier((absorbed, query))

    words = (half // HD) * QROWS
    away = struct((KVH, half + PAIR, HD), bf16)
    away, value, mine = call(
        front_kernel,
        [away, struct((KVH, half, HD), bf16), struct((KVH, PAIR, HD), bf16)],
        [H] * 6,
        [
            S(block_owner.shape[1:], jnp.int32),
            S(cache_len.shape, jnp.int32),
            V(query.shape, bf16),
            V(cache_kv.shape[1:], bf16),
            V(acts.shape, bf16),
            V((width, COLS), bf16),
            dma((7,)),
        ],
        flops=1_500_000_000,
        moved=6_000_000,
        limit=FRONT,
    )(block_owner[0], cache_len, own_query, cache_kv[0], acts, kv_weight)
    theirs = lax.ppermute(away, "core", swap)
    asked, value = lax.optimization_barrier((asked, value))
    score = call(
        other_kernel,
        struct((KVH, words, HD), bf16),
        [V, V],
        flops=140_000_000,
        moved=1_000_000,
    )(asked, acts)
    score = lax.ppermute(score, "core", swap)
    own = call(
        own_kernel,
        struct((KVH * QROWS, half), f32),
        [V, V],
        flops=10_000_000_000,
        moved=2_000_000,
    )(asked, acts)
    sent = call(
        pack_kernel,
        struct((KVH, half + (half // HD) * QROWS + PAIR, HD), bf16),
        [V] * 5,
        flops=10_000_000,
        moved=5_000_000,
    )(theirs, score, value, own, mine)
    got = lax.all_to_all(sent, "yx", 0, 0, tiled=True)

    parts = call(
        span_kernel,
        struct((2, 2 * n_yx, PAIR, HD), bf16),
        [V, V, V],
        flops=20_000_000,
        moved=3_000_000,
    )(got, query, draft_kv[0])
    parts = lax.all_to_all(
        parts.reshape(4 * n_yx, PAIR, HD), ("role", "yx", "core"), 0, 0, tiled=True
    )
    joined = call(
        join_kernel, struct((rows, KVH, QROWS, HD), bf16), [S, V], flops=10_000_000, moved=700_000
    )(span_row, parts.reshape(2, 2 * n_yx, PAIR, HD))
    output = joined.reshape(rows, KVH, GROUP, DRAFT, HD).transpose(0, 3, 1, 2, 4)
    return output.reshape(1, rows, DRAFT, QH * HD)


def solution(mesh):
    roles, groups, tps = mesh.devices.shape
    fine = Mesh(mesh.devices.reshape(roles, groups, tps // 2, 2), ("role", "grp", "yx", "core"))
    tp = ("yx", "core")
    placed = (
        P("role", "grp", None, tp),
        P(tp, None),
        P("role", "grp", tp, None),
        P("role", "grp"),
        P("role", "grp", None),
        P("role", "grp"),
        P("role", "grp", None, None),
        P("role", "grp", None, None),
    )
    return jax.shard_map(
        shards, mesh=fine, in_specs=placed, out_specs=P("role", "grp", None, None), check_vma=False
    )
```

```python
import functools
import math

import jax
import jax.numpy as jnp
from jax import lax
from jax.experimental import pallas as pl
from jax.experimental.pallas import tpu as pltpu
from jax.sharding import Mesh
from jax.sharding import PartitionSpec as P

QH = 64
KVH = 8
HD = 128
DRAFT = 4
GROUP = QH // KVH
QROWS = GROUP * DRAFT
STAT = 16
PAIR = QROWS + STAT
COLS = KVH * HD
NEG = -1e30
SCALE = 1.0 / math.sqrt(HD)

f32 = jnp.float32
bf16 = jnp.bfloat16


def dot_nt(a, b):
    return lax.dot_general(a, b, (((1,), (1,)), ((), ())), preferred_element_type=f32)


def dot_nn(a, b):
    return jnp.dot(a, b, preferred_element_type=f32)


def terms(lse):
    hi = lse.astype(bf16).astype(f32)
    mid = (lse - hi).astype(bf16).astype(f32)
    return hi, mid, lse - hi - mid


def packed_stat(lse):
    lane = lax.broadcasted_iota(jnp.int32, (QROWS, HD), 1)
    tile = jnp.zeros((QROWS, HD), f32)
    for at, term in enumerate(terms(lse)):
        tile = jnp.where(lane == at, term, tile)
    rows = tile.T[:STAT]
    return jnp.concatenate([rows, jnp.zeros((STAT, HD - QROWS), f32)], axis=1).astype(bf16)


def stat_row(tile):
    rows = tile.astype(f32)
    return rows[0:1] + rows[1:2] + rows[2:3]


def columns(rows):
    count = rows.shape[0]
    square = jnp.concatenate([rows, jnp.zeros((HD - count, HD), f32)], axis=0).T
    return [square[:QROWS, k : k + 1] for k in range(count)]


def attend(score, value):
    top = jnp.max(score, axis=-1, keepdims=True)
    weight = jnp.where(score > 0.5 * NEG, jnp.exp(score - top), 0.0)
    total = jnp.sum(weight, axis=-1, keepdims=True)
    any_key = total > 0.0
    safe = jnp.where(any_key, total, 1.0)
    out = dot_nn(weight.astype(bf16), value) / safe
    return out, jnp.where(any_key, top + jnp.log(safe), NEG)


def shares(rows):
    top = functools.reduce(jnp.maximum, rows)
    weights = [jnp.where(row > 0.5 * NEG, jnp.exp(row - top), 0.0) for row in rows]
    total = functools.reduce(jnp.add, weights)
    safe = jnp.where(total > 0.0, total, 1.0)
    return [w / safe for w in weights], jnp.where(total > 0.0, top + jnp.log(safe), NEG)


def stacked(parts):
    return jnp.concatenate(parts, axis=0)


def head_cols(head, start=0):
    return slice(start + head * HD, start + (head + 1) * HD)


def put_pair(out_ref, start, out, lse):
    middle = start + QROWS
    out_ref[:, start:middle] = out.astype(bf16).reshape(KVH, QROWS, HD)
    for head in range(KVH):
        out_ref[head, middle : middle + STAT] = packed_stat(
            lse[head * QROWS : (head + 1) * QROWS]
        )


def front_kernel(
    owner_hbm,
    len_hbm,
    q_hbm,
    cache_hbm,
    acts_hbm,
    w_hbm,
    away_hbm,
    value_hbm,
    mine_hbm,
    owner_ref,
    len_ref,
    q_ref,
    cache_ref,
    acts_ref,
    w_ref,
    value_ref,
    pair_ref,
    sems,
):
    core = lax.axis_index("core")
    me = lax.axis_index("yx") * 2 + core
    slab = cache_ref.shape[1]
    span = acts_ref.shape[0]
    half = span // 2
    order = (1 - core, core)
    early = [
        pltpu.make_async_copy(acts_hbm, acts_ref, sems.at[5]),
        pltpu.make_async_copy(w_hbm.at[:, COLS : 2 * COLS], w_ref, sems.at[6]),
    ]
    loads = [
        pltpu.make_async_copy(owner_hbm, owner_ref, sems.at[0]),
        pltpu.make_async_copy(len_hbm, len_ref, sems.at[1]),
        pltpu.make_async_copy(q_hbm, q_ref, sems.at[2]),
    ]
    loads += [
        pltpu.make_async_copy(cache_hbm.at[row], cache_ref.at[k], sems.at[3 + k])
        for k, row in enumerate(order)
    ]
    stores = [
        pltpu.make_async_copy(value_ref.at[0], away_hbm.at[:, :half], sems.at[7]),
        pltpu.make_async_copy(value_ref.at[1], value_hbm, sems.at[8]),
        pltpu.make_async_copy(pair_ref.at[0], away_hbm.at[:, half : half + PAIR], sems.at[9]),
        pltpu.make_async_copy(pair_ref.at[1], mine_hbm, sems.at[10]),
    ]
    for copy in (*early, *loads):
        copy.start()
    for copy in early:
        copy.wait()
    for k, row in enumerate(order):
        tokens = acts_ref[pl.ds(pl.multiple_of(row * half, half), half), :]
        value = dot_nn(tokens, w_ref[...]).astype(bf16)
        for head in range(KVH):
            value_ref[k, head] = value[:, head_cols(head)]
        stores[k].start()
    for copy in loads:
        copy.wait()
    lives = []
    for row in order:
        first = jnp.int32(0)
        for block in range(owner_ref.shape[1]):
            first = first + jnp.where(owner_ref[row, block] == me, block, 0)
        room = len_ref[0, row] - first * slab
        lives.append(lax.broadcasted_iota(jnp.int32, (KVH * QROWS, slab), 1) < room)
    live = stacked(lives)
    places = [(k, row, head) for k, row in enumerate(order) for head in range(KVH)]
    score = stacked(
        [dot_nt(q_ref[row, head], cache_ref[k, :, head_cols(head)]) for k, row, head in places]
    )
    score = jnp.where(live, score * SCALE, NEG)
    top = jnp.max(score, axis=-1, keepdims=True)
    weight = jnp.where(live, jnp.exp(score - top), 0.0)
    total = jnp.sum(weight, axis=-1, keepdims=True)
    safe = jnp.where(total > 0.0, total, 1.0)
    weight = weight.astype(bf16)
    out = stacked(
        [
            dot_nn(
                weight[at * QROWS : (at + 1) * QROWS], cache_ref[k, :, head_cols(head, COLS)]
            )
            for at, (k, _, head) in enumerate(places)
        ]
    )
    out = out / safe
    lse = jnp.where(total > 0.0, top + jnp.log(safe), NEG)
    middle = KVH * QROWS
    put_pair(pair_ref.at[0], 0, out[:middle], lse[:middle])
    put_pair(pair_ref.at[1], 0, out[middle:], lse[middle:])
    for store in stores[2:]:
        store.start()
    for store in stores:
        store.wait()


def absorb_kernel(span_ref, q_hbm, w_hbm, out_ref, q_ref, w_ref, sems):
    middle = COLS // 2
    row = span_ref[0, 0]
    first = pltpu.make_async_copy(q_hbm.at[row], q_ref, sems.at[2])
    loads = [
        pltpu.make_async_copy(w_hbm.at[:, cols], w_ref.at[:, cols], sems.at[k])
        for k, cols in enumerate((slice(0, middle), slice(middle, COLS)))
    ]
    for copy in (first, *loads):
        copy.start()
    first.wait()
    for head in range(KVH):
        if head * HD % middle == 0:
            loads[head * HD // middle].wait()
        rows = slice(head * QROWS, (head + 1) * QROWS)
        out_ref[rows] = dot_nt(q_ref[head], w_ref[:, head_cols(head)]).astype(bf16)


def other_kernel(qw_ref, acts_ref, out_ref):
    half = acts_ref.shape[0] // 2
    start = pl.multiple_of((1 - lax.axis_index("core")) * half, half)
    score = (dot_nt(qw_ref[...], acts_ref[pl.ds(start, half), :]) * SCALE).astype(bf16)
    for tile in range(half // HD):
        at = tile * QROWS
        out_ref[:, at : at + QROWS] = score[:, head_cols(tile)].reshape(KVH, QROWS, HD)


def own_kernel(qw_ref, acts_ref, own_ref):
    half = acts_ref.shape[0] // 2
    start = pl.multiple_of(lax.axis_index("core") * half, half)
    own_ref[...] = dot_nt(qw_ref[...], acts_ref[pl.ds(start, half), :]) * SCALE


def pack_kernel(got_ref, score_ref, value_ref, own_ref, mine_ref, out_ref):
    half = value_ref.shape[1]
    tiles = half // HD
    out_ref[:, :half] = (value_ref[...].astype(f32) + got_ref[:, :half].astype(f32)).astype(bf16)
    shape = (KVH, QROWS, HD)
    for tile in range(tiles):
        at = tile * QROWS
        score = own_ref[:, head_cols(tile)].reshape(shape)
        score = score + score_ref[:, at : at + QROWS].astype(f32)
        at = half + at
        out_ref[:, at : at + QROWS] = score.astype(bf16)
    at = half + tiles * QROWS
    middle = at + QROWS
    pair = [
        [stat_row(ref[head, first : first + STAT]) for head in range(KVH)]
        for ref, first in ((mine_ref, QROWS), (got_ref, half + QROWS))
    ]
    weights, lse = shares([stacked(rows) for rows in pair])
    weights = columns(stacked(weights))
    packed = [jnp.concatenate(terms(lse[head : head + 1]), axis=0) for head in range(KVH)]
    for head in range(KVH):
        out_ref[head, at:middle] = (
            weights[head] * mine_ref[head, :QROWS].astype(f32)
            + weights[KVH + head] * got_ref[head, half : half + QROWS].astype(f32)
        ).astype(bf16)
        out_ref[head, middle : middle + STAT] = jnp.concatenate(
            [packed[head], jnp.zeros((STAT - 3, HD), f32)], axis=0
        ).astype(bf16)


def span_kernel(got_ref, q_ref, draft_ref, out_ref):
    parts, length, _ = got_ref.shape
    half = (length - PAIR) * HD // (HD + QROWS)
    tiles = half // HD
    role = lax.axis_index("role")
    core = lax.axis_index("core")
    head = lax.axis_index("yx")

    def total(start, size):
        acc = got_ref[0, start : start + size].astype(f32)
        for part in range(1, parts):
            acc = acc + got_ref[part, start : start + size].astype(f32)
        return acc

    value = total(0, half).astype(bf16)
    score = jnp.concatenate(
        [total(half + tile * QROWS, QROWS) for tile in range(tiles)], axis=1
    )
    out, lse = attend(score, value)
    fresh = stacked([out.astype(bf16), packed_stat(lse)])

    query = q_ref[core, head]
    start = pl.multiple_of(head * HD, HD)
    draft_keys = draft_ref[core, :, pl.ds(start, HD)].astype(f32)
    draft_vals = draft_ref[core, :, pl.ds(start + COLS, HD)].astype(f32)
    token = lax.broadcasted_iota(jnp.int32, (QROWS, 1), 0) % DRAFT
    scores = []
    for u in range(DRAFT):
        one = jnp.sum(query.astype(f32) * draft_keys[u : u + 1], axis=-1, keepdims=True) * SCALE
        scores.append(jnp.where(token >= u, one, NEG))
    top = functools.reduce(jnp.maximum, scores)
    weights = [jnp.where(one > 0.5 * NEG, jnp.exp(one - top), 0.0) for one in scores]
    sums = functools.reduce(jnp.add, weights)
    drafted = functools.reduce(
        jnp.add,
        [w.astype(bf16).astype(f32) * draft_vals[u : u + 1] for u, w in enumerate(weights)],
    )
    at = half + tiles * QROWS
    middle = at + QROWS
    rows = [stat_row(got_ref[part, middle : middle + STAT]) for part in range(parts)]
    rows.append(stat_row(packed_stat(top + jnp.log(sums))))
    weights, lse = shares(rows)
    weights = columns(stacked(weights))
    out = weights[parts] * (drafted / sums)
    for part in range(parts):
        out = out + weights[part] * got_ref[part, at:middle].astype(f32)
    spare = jnp.zeros((STAT - 3, HD), f32)
    kept = stacked([out.astype(bf16), stacked([*terms(lse), spare]).astype(bf16)])

    chunks = out_ref.shape[1]
    for chunk in range(chunks):
        out_ref[role, chunk] = kept
        out_ref[1 - role, chunk] = fresh


def join_kernel(span_ref, got_ref, out_hbm, out_ref, sems):
    role = lax.axis_index("role")
    rows = out_ref.shape[0]
    stores = [
        pltpu.make_async_copy(out_ref.at[row], out_hbm.at[row], sems.at[row])
        for row in range(rows)
    ]

    def stats(pool, core):
        return stacked([stat_row(got_ref[pool, 2 * head + core, QROWS:]) for head in range(KVH)])

    fresh = [stats(1 - role, core) for core in range(2)]
    weights = []
    for row in range(rows):
        taken = span_ref[0, 0] == row
        kept = [jnp.where(taken, lse, NEG) for lse in fresh]
        weights += shares([stats(role, row), *kept])[0]
    weights = columns(stacked(weights))
    for row in range(rows):
        for head in range(KVH):
            sources = [(role, row), (1 - role, 0), (1 - role, 1)]
            out = jnp.zeros((QROWS, HD), f32)
            for k, (pool, core) in enumerate(sources):
                weight = weights[(row * 3 + k) * KVH + head]
                out = out + weight * got_ref[pool, 2 * head + core, :QROWS].astype(f32)
            out_ref[row, head] = out.astype(bf16)
        stores[row].start()
    for store in stores:
        store.wait()


def call(kernel, out_shapes, spaces, scratch=(), flops=0, moved=0, limit=24, out_space=pltpu.VMEM):
    out_specs = jax.tree.map(lambda _: pl.BlockSpec(memory_space=out_space), out_shapes)
    return pl.pallas_call(
        kernel,
        out_shape=out_shapes,
        in_specs=[pl.BlockSpec(memory_space=space) for space in spaces],
        out_specs=out_specs,
        scratch_shapes=list(scratch),
        compiler_params=pltpu.CompilerParams(vmem_limit_bytes=limit << 20),
        cost_estimate=pl.CostEstimate(flops=flops, bytes_accessed=moved, transcendentals=0),
    )


V = pltpu.VMEM
S = pltpu.SMEM
H = pltpu.HBM
FRONT = 58


def shards(
    prompt_acts, kv_weight, cache_kv, cache_len, block_owner, span_row, draft_query, draft_kv
):
    swap = [(0, 1), (1, 0)]
    acts = prompt_acts[0, 0]
    span, width = acts.shape
    half = span // 2
    rows = cache_kv.shape[1]
    n_yx = lax.axis_size("yx")
    struct = jax.ShapeDtypeStruct

    query = draft_query[0].reshape(rows, DRAFT, KVH, GROUP, HD).transpose(0, 2, 3, 1, 4)
    query = query.reshape(rows, KVH, QROWS, HD)
    dma = pltpu.SemaphoreType.DMA
    absorbed = call(
        absorb_kernel,
        struct((KVH * QROWS, width), bf16),
        [S, H, H],
        [V(query.shape[1:], bf16), V((width, COLS), bf16), dma((3,))],
        flops=70_000_000,
        moved=1_500_000,
        limit=FRONT,
    )(span_row, query, kv_weight)
    asked = lax.ppermute(absorbed, "role", swap)
    absorbed, own_query = lax.optimization_barrier((absorbed, query))

    words = (half // HD) * QROWS
    away = struct((KVH, half + PAIR, HD), bf16)
    away, value, mine = call(
        front_kernel,
        [away, struct((KVH, half, HD), bf16), struct((KVH, PAIR, HD), bf16)],
        [H] * 6,
        [
            S(block_owner.shape[1:], jnp.int32),
            S(cache_len.shape, jnp.int32),
            V(query.shape, bf16),
            V(cache_kv.shape[1:], bf16),
            V(acts.shape, bf16),
            V((width, COLS), bf16),
            V((2, KVH, half, HD), bf16),
            V((2, KVH, PAIR, HD), bf16),
            dma((11,)),
        ],
        flops=1_500_000_000,
        moved=6_000_000,
        limit=FRONT,
        out_space=H,
    )(block_owner[0], cache_len, own_query, cache_kv[0], acts, kv_weight)
    theirs = lax.ppermute(away, "core", swap)
    asked, value = lax.optimization_barrier((asked, value))
    score = call(
        other_kernel,
        struct((KVH, words, HD), bf16),
        [V, V],
        flops=140_000_000,
        moved=1_000_000,
    )(asked, acts)
    score = lax.ppermute(score, "core", swap)
    own = call(
        own_kernel,
        struct((KVH * QROWS, half), f32),
        [V, V],
        flops=10_000_000_000,
        moved=2_000_000,
    )(asked, acts)
    sent = call(
        pack_kernel,
        struct((KVH, half + (half // HD) * QROWS + PAIR, HD), bf16),
        [V] * 5,
        flops=10_000_000,
        moved=5_000_000,
    )(theirs, score, value, own, mine)
    got = lax.all_to_all(sent, "yx", 0, 0, tiled=True)

    parts = call(
        span_kernel,
        struct((2, 2 * n_yx, PAIR, HD), bf16),
        [V, V, V],
        flops=20_000_000,
        moved=3_000_000,
    )(got, query, draft_kv[0])
    parts = lax.all_to_all(
        parts.reshape(4 * n_yx, PAIR, HD), ("role", "yx", "core"), 0, 0, tiled=True
    )
    joined = struct((rows, KVH, QROWS, HD), bf16)
    joined = call(
        join_kernel,
        joined,
        [S, V],
        [V(joined.shape, bf16), dma((rows,))],
        flops=10_000_000,
        moved=700_000,
        out_space=H,
    )(span_row, parts.reshape(2, 2 * n_yx, PAIR, HD))
    output = joined.reshape(rows, KVH, GROUP, DRAFT, HD).transpose(0, 3, 1, 2, 4)
    return output.reshape(1, rows, DRAFT, QH * HD)


def solution(mesh):
    roles, groups, tps = mesh.devices.shape
    fine = Mesh(mesh.devices.reshape(roles, groups, tps // 2, 2), ("role", "grp", "yx", "core"))
    tp = ("yx", "core")
    placed = (
        P("role", "grp", None, tp),
        P(tp, None),
        P("role", "grp", tp, None),
        P("role", "grp"),
        P("role", "grp", None),
        P("role", "grp"),
        P("role", "grp", None, None),
        P("role", "grp", None, None),
    )
    return jax.shard_map(
        shards, mesh=fine, in_specs=placed, out_specs=P("role", "grp", None, None), check_vma=False
    )
```

```python
import functools
import math

import jax
import jax.numpy as jnp
from jax import lax
from jax.experimental import pallas as pl
from jax.experimental.pallas import tpu as pltpu
from jax.sharding import Mesh
from jax.sharding import PartitionSpec as P

QH = 64
KVH = 8
HD = 128
DRAFT = 4
GROUP = QH // KVH
QROWS = GROUP * DRAFT
STAT = 16
PARTS = 4
PAIR = QROWS + STAT
COLS = KVH * HD
NEG = -1e30
SCALE = 1.0 / math.sqrt(HD)

f32 = jnp.float32
bf16 = jnp.bfloat16


def dot_nt(a, b):
    return lax.dot_general(a, b, (((1,), (1,)), ((), ())), preferred_element_type=f32)


def dot_nn(a, b):
    return jnp.dot(a, b, preferred_element_type=f32)


def terms(lse):
    hi = lse.astype(bf16).astype(f32)
    mid = (lse - hi).astype(bf16).astype(f32)
    return hi, mid, lse - hi - mid


def packed_stat(lse):
    lane = lax.broadcasted_iota(jnp.int32, (QROWS, HD), 1)
    tile = jnp.zeros((QROWS, HD), f32)
    for at, term in enumerate(terms(lse)):
        tile = jnp.where(lane == at, term, tile)
    rows = tile.T[:STAT]
    return jnp.concatenate([rows, jnp.zeros((STAT, HD - QROWS), f32)], axis=1).astype(bf16)


def stat_row(tile):
    rows = tile.astype(f32)
    return rows[0:1] + rows[1:2] + rows[2:3]


def columns(rows):
    count = rows.shape[0]
    square = jnp.concatenate([rows, jnp.zeros((HD - count, HD), f32)], axis=0).T
    return [square[:QROWS, k : k + 1] for k in range(count)]


def attend(score, value):
    top = jnp.max(score, axis=-1, keepdims=True)
    weight = jnp.where(score > 0.5 * NEG, jnp.exp(score - top), 0.0)
    total = jnp.sum(weight, axis=-1, keepdims=True)
    any_key = total > 0.0
    safe = jnp.where(any_key, total, 1.0)
    out = dot_nn(weight.astype(bf16), value) / safe
    return out, jnp.where(any_key, top + jnp.log(safe), NEG)


def shares(rows):
    top = functools.reduce(jnp.maximum, rows)
    weights = [jnp.where(row > 0.5 * NEG, jnp.exp(row - top), 0.0) for row in rows]
    total = functools.reduce(jnp.add, weights)
    safe = jnp.where(total > 0.0, total, 1.0)
    return [w / safe for w in weights], jnp.where(total > 0.0, top + jnp.log(safe), NEG)


def stacked(parts):
    return jnp.concatenate(parts, axis=0)


def head_cols(head, start=0):
    return slice(start + head * HD, start + (head + 1) * HD)


def put_pair(out_ref, start, out, lse):
    middle = start + QROWS
    out_ref[:, start:middle] = out.astype(bf16).reshape(KVH, QROWS, HD)
    for head in range(KVH):
        out_ref[head, middle : middle + STAT] = packed_stat(
            lse[head * QROWS : (head + 1) * QROWS]
        )


def front_kernel(
    owner_hbm,
    len_hbm,
    q_hbm,
    cache_hbm,
    acts_hbm,
    w_hbm,
    away_hbm,
    value_hbm,
    mine_hbm,
    owner_ref,
    len_ref,
    q_ref,
    cache_ref,
    acts_ref,
    w_ref,
    value_ref,
    pair_ref,
    sems,
):
    core = lax.axis_index("core")
    me = lax.axis_index("yx") * 2 + core
    slab = cache_ref.shape[1]
    span = acts_ref.shape[0]
    half = span // 2
    order = (1 - core, core)
    early = [
        pltpu.make_async_copy(acts_hbm, acts_ref, sems.at[5]),
        pltpu.make_async_copy(w_hbm.at[:, COLS : 2 * COLS], w_ref, sems.at[6]),
    ]
    loads = [
        pltpu.make_async_copy(owner_hbm, owner_ref, sems.at[0]),
        pltpu.make_async_copy(len_hbm, len_ref, sems.at[1]),
        pltpu.make_async_copy(q_hbm, q_ref, sems.at[2]),
    ]
    loads += [
        pltpu.make_async_copy(cache_hbm.at[row], cache_ref.at[k], sems.at[3 + k])
        for k, row in enumerate(order)
    ]
    stores = [
        pltpu.make_async_copy(value_ref.at[0], away_hbm.at[:, :half], sems.at[7]),
        pltpu.make_async_copy(value_ref.at[1], value_hbm, sems.at[8]),
        pltpu.make_async_copy(pair_ref.at[0], away_hbm.at[:, half : half + PAIR], sems.at[9]),
        pltpu.make_async_copy(pair_ref.at[1], mine_hbm, sems.at[10]),
    ]
    for copy in (*early, *loads):
        copy.start()
    for copy in early:
        copy.wait()

    def values(k):
        start = pl.multiple_of(order[k] * half, half)
        value = dot_nn(acts_ref[pl.ds(start, half), :], w_ref[...]).astype(bf16)
        for head in range(KVH):
            value_ref[k, head] = value[:, head_cols(head)]
        stores[k].start()

    values(0)
    for copy in loads:
        copy.wait()
    lives = []
    for row in order:
        first = jnp.int32(0)
        for block in range(owner_ref.shape[1]):
            first = first + jnp.where(owner_ref[row, block] == me, block, 0)
        room = len_ref[0, row] - first * slab
        lives.append(lax.broadcasted_iota(jnp.int32, (KVH * QROWS, slab), 1) < room)
    live = stacked(lives)
    places = [(k, row, head) for k, row in enumerate(order) for head in range(KVH)]
    score = stacked(
        [dot_nt(q_ref[row, head], cache_ref[k, :, head_cols(head)]) for k, row, head in places]
    )
    values(1)
    score = jnp.where(live, score * SCALE, NEG)
    top = jnp.max(score, axis=-1, keepdims=True)
    weight = jnp.where(live, jnp.exp(score - top), 0.0)
    total = jnp.sum(weight, axis=-1, keepdims=True)
    safe = jnp.where(total > 0.0, total, 1.0)
    weight = weight.astype(bf16)
    out = stacked(
        [
            dot_nn(
                weight[at * QROWS : (at + 1) * QROWS], cache_ref[k, :, head_cols(head, COLS)]
            )
            for at, (k, _, head) in enumerate(places)
        ]
    )
    out = out / safe
    lse = jnp.where(total > 0.0, top + jnp.log(safe), NEG)
    middle = KVH * QROWS
    put_pair(pair_ref.at[0], 0, out[:middle], lse[:middle])
    put_pair(pair_ref.at[1], 0, out[middle:], lse[middle:])
    for store in stores[2:]:
        store.start()
    for store in stores:
        store.wait()


def absorb_kernel(span_ref, q_hbm, w_hbm, out_ref, q_ref, w_ref, sems):
    part = COLS // PARTS
    row = span_ref[0, 0]
    first = pltpu.make_async_copy(q_hbm.at[row], q_ref, sems.at[PARTS])
    loads = [
        pltpu.make_async_copy(w_hbm.at[:, cols], w_ref.at[:, cols], sems.at[k])
        for k, cols in enumerate(slice(k * part, (k + 1) * part) for k in range(PARTS))
    ]
    for copy in (first, *loads):
        copy.start()
    first.wait()
    for head in range(KVH):
        if head * HD % part == 0:
            loads[head * HD // part].wait()
        rows = slice(head * QROWS, (head + 1) * QROWS)
        out_ref[rows] = dot_nt(q_ref[head], w_ref[:, head_cols(head)]).astype(bf16)


def other_kernel(qw_ref, acts_ref, out_ref):
    half = acts_ref.shape[0] // 2
    start = pl.multiple_of((1 - lax.axis_index("core")) * half, half)
    score = (dot_nt(qw_ref[...], acts_ref[pl.ds(start, half), :]) * SCALE).astype(bf16)
    for tile in range(half // HD):
        at = tile * QROWS
        out_ref[:, at : at + QROWS] = score[:, head_cols(tile)].reshape(KVH, QROWS, HD)


def own_kernel(qw_ref, acts_ref, own_ref):
    half = acts_ref.shape[0] // 2
    start = pl.multiple_of(lax.axis_index("core") * half, half)
    own_ref[...] = dot_nt(qw_ref[...], acts_ref[pl.ds(start, half), :]) * SCALE


def pack_kernel(got_ref, score_ref, value_ref, own_ref, mine_ref, out_ref):
    half = value_ref.shape[1]
    tiles = half // HD
    out_ref[:, :half] = value_ref[...] + got_ref[:, :half]
    shape = (KVH, QROWS, HD)
    for tile in range(tiles):
        at = tile * QROWS
        score = own_ref[:, head_cols(tile)].reshape(shape)
        score = score + score_ref[:, at : at + QROWS].astype(f32)
        at = half + at
        out_ref[:, at : at + QROWS] = score.astype(bf16)
    at = half + tiles * QROWS
    middle = at + QROWS
    pair = [
        [stat_row(ref[head, first : first + STAT]) for head in range(KVH)]
        for ref, first in ((mine_ref, QROWS), (got_ref, half + QROWS))
    ]
    weights, lse = shares([stacked(rows) for rows in pair])
    weights = columns(stacked(weights))
    packed = [jnp.concatenate(terms(lse[head : head + 1]), axis=0) for head in range(KVH)]
    for head in range(KVH):
        out_ref[head, at:middle] = (
            weights[head] * mine_ref[head, :QROWS].astype(f32)
            + weights[KVH + head] * got_ref[head, half : half + QROWS].astype(f32)
        ).astype(bf16)
        out_ref[head, middle : middle + STAT] = jnp.concatenate(
            [packed[head], jnp.zeros((STAT - 3, HD), f32)], axis=0
        ).astype(bf16)


def span_kernel(got_ref, q_ref, draft_ref, out_ref):
    parts, length, _ = got_ref.shape
    half = (length - PAIR) * HD // (HD + QROWS)
    tiles = half // HD
    role = lax.axis_index("role")
    core = lax.axis_index("core")
    head = lax.axis_index("yx")

    def total(start, size):
        acc = got_ref[0, start : start + size].astype(f32)
        for part in range(1, parts):
            acc = acc + got_ref[part, start : start + size].astype(f32)
        return acc

    value = total(0, half).astype(bf16)
    score = jnp.concatenate(
        [total(half + tile * QROWS, QROWS) for tile in range(tiles)], axis=1
    )
    out, lse = attend(score, value)
    fresh = stacked([out.astype(bf16), packed_stat(lse)])

    query = q_ref[core, head]
    start = pl.multiple_of(head * HD, HD)
    draft_keys = draft_ref[core, :, pl.ds(start, HD)].astype(f32)
    draft_vals = draft_ref[core, :, pl.ds(start + COLS, HD)].astype(f32)
    token = lax.broadcasted_iota(jnp.int32, (QROWS, 1), 0) % DRAFT
    scores = []
    for u in range(DRAFT):
        one = jnp.sum(query.astype(f32) * draft_keys[u : u + 1], axis=-1, keepdims=True) * SCALE
        scores.append(jnp.where(token >= u, one, NEG))
    top = functools.reduce(jnp.maximum, scores)
    weights = [jnp.where(one > 0.5 * NEG, jnp.exp(one - top), 0.0) for one in scores]
    sums = functools.reduce(jnp.add, weights)
    drafted = functools.reduce(
        jnp.add,
        [w.astype(bf16).astype(f32) * draft_vals[u : u + 1] for u, w in enumerate(weights)],
    )
    at = half + tiles * QROWS
    middle = at + QROWS
    rows = [stat_row(got_ref[part, middle : middle + STAT]) for part in range(parts)]
    rows.append(stat_row(packed_stat(top + jnp.log(sums))))
    weights, lse = shares(rows)
    weights = columns(stacked(weights))
    out = weights[parts] * (drafted / sums)
    for part in range(parts):
        out = out + weights[part] * got_ref[part, at:middle].astype(f32)
    spare = jnp.zeros((STAT - 3, HD), f32)
    kept = stacked([out.astype(bf16), stacked([*terms(lse), spare]).astype(bf16)])

    chunks = out_ref.shape[1]
    for chunk in range(chunks):
        out_ref[role, chunk] = kept
        out_ref[1 - role, chunk] = fresh


def join_kernel(span_ref, got_ref, out_hbm, out_ref, sems):
    role = lax.axis_index("role")
    rows = out_ref.shape[0]
    stores = [
        pltpu.make_async_copy(out_ref.at[row], out_hbm.at[row], sems.at[row])
        for row in range(rows)
    ]

    def stats(pool, core):
        return stacked([stat_row(got_ref[pool, 2 * head + core, QROWS:]) for head in range(KVH)])

    fresh = [stats(1 - role, core) for core in range(2)]
    weights = []
    for row in range(rows):
        taken = span_ref[0, 0] == row
        kept = [jnp.where(taken, lse, NEG) for lse in fresh]
        weights += shares([stats(role, row), *kept])[0]
    weights = columns(stacked(weights))
    for row in range(rows):
        for head in range(KVH):
            sources = [(role, row), (1 - role, 0), (1 - role, 1)]
            out = jnp.zeros((QROWS, HD), f32)
            for k, (pool, core) in enumerate(sources):
                weight = weights[(row * 3 + k) * KVH + head]
                out = out + weight * got_ref[pool, 2 * head + core, :QROWS].astype(f32)
            out_ref[row, head] = out.astype(bf16)
        stores[row].start()
    for store in stores:
        store.wait()


def call(kernel, out_shapes, spaces, scratch=(), flops=0, moved=0, limit=24, out_space=pltpu.VMEM):
    out_specs = jax.tree.map(lambda _: pl.BlockSpec(memory_space=out_space), out_shapes)
    return pl.pallas_call(
        kernel,
        out_shape=out_shapes,
        in_specs=[pl.BlockSpec(memory_space=space) for space in spaces],
        out_specs=out_specs,
        scratch_shapes=list(scratch),
        compiler_params=pltpu.CompilerParams(vmem_limit_bytes=limit << 20),
        cost_estimate=pl.CostEstimate(flops=flops, bytes_accessed=moved, transcendentals=0),
    )


V = pltpu.VMEM
S = pltpu.SMEM
H = pltpu.HBM
FRONT = 58


def shards(
    prompt_acts, kv_weight, cache_kv, cache_len, block_owner, span_row, draft_query, draft_kv
):
    swap = [(0, 1), (1, 0)]
    acts = prompt_acts[0, 0]
    span, width = acts.shape
    half = span // 2
    rows = cache_kv.shape[1]
    n_yx = lax.axis_size("yx")
    struct = jax.ShapeDtypeStruct

    query = draft_query[0].reshape(rows, DRAFT, KVH, GROUP, HD).transpose(0, 2, 3, 1, 4)
    query = query.reshape(rows, KVH, QROWS, HD)
    dma = pltpu.SemaphoreType.DMA
    absorbed = call(
        absorb_kernel,
        struct((KVH * QROWS, width), bf16),
        [S, H, H],
        [V(query.shape[1:], bf16), V((width, COLS), bf16), dma((PARTS + 1,))],
        flops=70_000_000,
        moved=1_500_000,
        limit=FRONT,
    )(span_row, query, kv_weight)
    asked = lax.ppermute(absorbed, "role", swap)
    absorbed, own_query = lax.optimization_barrier((absorbed, query))

    words = (half // HD) * QROWS
    away = struct((KVH, half + PAIR, HD), bf16)
    away, value, mine = call(
        front_kernel,
        [away, struct((KVH, half, HD), bf16), struct((KVH, PAIR, HD), bf16)],
        [H] * 6,
        [
            S(block_owner.shape[1:], jnp.int32),
            S(cache_len.shape, jnp.int32),
            V(query.shape, bf16),
            V(cache_kv.shape[1:], bf16),
            V(acts.shape, bf16),
            V((width, COLS), bf16),
            V((2, KVH, half, HD), bf16),
            V((2, KVH, PAIR, HD), bf16),
            dma((11,)),
        ],
        flops=1_500_000_000,
        moved=6_000_000,
        limit=FRONT,
        out_space=H,
    )(block_owner[0], cache_len, own_query, cache_kv[0], acts, kv_weight)
    theirs = lax.ppermute(away, "core", swap)
    asked, value = lax.optimization_barrier((asked, value))
    score = call(
        other_kernel,
        struct((KVH, words, HD), bf16),
        [V, V],
        flops=140_000_000,
        moved=1_000_000,
    )(asked, acts)
    score = lax.ppermute(score, "core", swap)
    own = call(
        own_kernel,
        struct((KVH * QROWS, half), f32),
        [V, V],
        flops=10_000_000_000,
        moved=2_000_000,
    )(asked, acts)
    sent = call(
        pack_kernel,
        struct((KVH, half + (half // HD) * QROWS + PAIR, HD), bf16),
        [V] * 5,
        flops=10_000_000,
        moved=5_000_000,
    )(theirs, score, value, own, mine)
    got = lax.all_to_all(sent, "yx", 0, 0, tiled=True)

    parts = call(
        span_kernel,
        struct((2, 2 * n_yx, PAIR, HD), bf16),
        [V, V, V],
        flops=20_000_000,
        moved=3_000_000,
    )(got, query, draft_kv[0])
    parts = lax.all_to_all(
        parts.reshape(4 * n_yx, PAIR, HD), ("role", "yx", "core"), 0, 0, tiled=True
    )
    joined = struct((rows, KVH, QROWS, HD), bf16)
    joined = call(
        join_kernel,
        joined,
        [S, V],
        [V(joined.shape, bf16), dma((rows,))],
        flops=10_000_000,
        moved=700_000,
        out_space=H,
    )(span_row, parts.reshape(2, 2 * n_yx, PAIR, HD))
    output = joined.reshape(rows, KVH, GROUP, DRAFT, HD).transpose(0, 3, 1, 2, 4)
    return output.reshape(1, rows, DRAFT, QH * HD)


def solution(mesh):
    roles, groups, tps = mesh.devices.shape
    fine = Mesh(mesh.devices.reshape(roles, groups, tps // 2, 2), ("role", "grp", "yx", "core"))
    tp = ("yx", "core")
    placed = (
        P("role", "grp", None, tp),
        P(tp, None),
        P("role", "grp", tp, None),
        P("role", "grp"),
        P("role", "grp", None),
        P("role", "grp"),
        P("role", "grp", None, None),
        P("role", "grp", None, None),
    )
    return jax.shard_map(
        shards, mesh=fine, in_specs=placed, out_specs=P("role", "grp", None, None), check_vma=False
    )
```

```python
import functools
import math

import jax
import jax.numpy as jnp
from jax import lax
from jax.experimental import pallas as pl
from jax.experimental.pallas import tpu as pltpu
from jax.sharding import Mesh
from jax.sharding import PartitionSpec as P

QH = 64
KVH = 8
HD = 128
DRAFT = 4
GROUP = QH // KVH
QROWS = GROUP * DRAFT
STAT = 16
PAIR = QROWS + STAT
COLS = KVH * HD
NEG = -1e30
SCALE = 1.0 / math.sqrt(HD)

f32 = jnp.float32
bf16 = jnp.bfloat16


def dot_nt(a, b):
    return lax.dot_general(a, b, (((1,), (1,)), ((), ())), preferred_element_type=f32)


def dot_nn(a, b):
    return jnp.dot(a, b, preferred_element_type=f32)


def terms(lse):
    hi = lse.astype(bf16).astype(f32)
    mid = (lse - hi).astype(bf16).astype(f32)
    return hi, mid, lse - hi - mid


def packed_stat(lse):
    lane = lax.broadcasted_iota(jnp.int32, (QROWS, HD), 1)
    tile = jnp.zeros((QROWS, HD), f32)
    for at, term in enumerate(terms(lse)):
        tile = jnp.where(lane == at, term, tile)
    rows = tile.T[:STAT]
    return jnp.concatenate([rows, jnp.zeros((STAT, HD - QROWS), f32)], axis=1).astype(bf16)


def stat_row(tile):
    rows = tile.astype(f32)
    return rows[0:1] + rows[1:2] + rows[2:3]


def columns(rows):
    count = rows.shape[0]
    square = jnp.concatenate([rows, jnp.zeros((HD - count, HD), f32)], axis=0).T
    return [square[:QROWS, k : k + 1] for k in range(count)]


def attend(score, value):
    top = jnp.max(score, axis=-1, keepdims=True)
    weight = jnp.where(score > 0.5 * NEG, jnp.exp(score - top), 0.0)
    total = jnp.sum(weight, axis=-1, keepdims=True)
    any_key = total > 0.0
    safe = jnp.where(any_key, total, 1.0)
    out = dot_nn(weight.astype(bf16), value) / safe
    return out, jnp.where(any_key, top + jnp.log(safe), NEG)


def shares(rows):
    top = functools.reduce(jnp.maximum, rows)
    weights = [jnp.where(row > 0.5 * NEG, jnp.exp(row - top), 0.0) for row in rows]
    total = functools.reduce(jnp.add, weights)
    safe = jnp.where(total > 0.0, total, 1.0)
    return [w / safe for w in weights], jnp.where(total > 0.0, top + jnp.log(safe), NEG)


def stacked(parts):
    return jnp.concatenate(parts, axis=0)


def head_cols(head, start=0):
    return slice(start + head * HD, start + (head + 1) * HD)


def put_pair(out_ref, start, out, lse):
    middle = start + QROWS
    out_ref[:, start:middle] = out.astype(bf16).reshape(KVH, QROWS, HD)
    for head in range(KVH):
        out_ref[head, middle : middle + STAT] = packed_stat(
            lse[head * QROWS : (head + 1) * QROWS]
        )


def front_kernel(
    owner_hbm,
    len_hbm,
    q_hbm,
    cache_hbm,
    acts_hbm,
    w_hbm,
    away_hbm,
    value_hbm,
    mine_hbm,
    owner_ref,
    len_ref,
    q_ref,
    cache_ref,
    acts_ref,
    w_ref,
    value_ref,
    pair_ref,
    sems,
):
    core = lax.axis_index("core")
    me = lax.axis_index("yx") * 2 + core
    slab = cache_ref.shape[1]
    half = acts_ref.shape[1]
    order = (1 - core, core)
    early = [pltpu.make_async_copy(w_hbm.at[:, COLS : 2 * COLS], w_ref, sems.at[6])]
    early += [
        pltpu.make_async_copy(
            acts_hbm.at[pl.ds(pl.multiple_of(row * half, half), half)], acts_ref.at[k], sems.at[at]
        )
        for k, (row, at) in enumerate(zip(order, (5, 11)))
    ]
    loads = [
        pltpu.make_async_copy(owner_hbm, owner_ref, sems.at[0]),
        pltpu.make_async_copy(len_hbm, len_ref, sems.at[1]),
        pltpu.make_async_copy(q_hbm, q_ref, sems.at[2]),
    ]
    loads += [
        pltpu.make_async_copy(cache_hbm.at[row], cache_ref.at[k], sems.at[3 + k])
        for k, row in enumerate(order)
    ]
    stores = [
        pltpu.make_async_copy(value_ref.at[0], away_hbm.at[:, :half], sems.at[7]),
        pltpu.make_async_copy(value_ref.at[1], value_hbm, sems.at[8]),
        pltpu.make_async_copy(pair_ref.at[0], away_hbm.at[:, half : half + PAIR], sems.at[9]),
        pltpu.make_async_copy(pair_ref.at[1], mine_hbm, sems.at[10]),
    ]
    for copy in (*early, *loads):
        copy.start()
    early[0].wait()
    for k in range(2):
        early[1 + k].wait()
        value = dot_nn(acts_ref[k], w_ref[...]).astype(bf16)
        for head in range(KVH):
            value_ref[k, head] = value[:, head_cols(head)]
        stores[k].start()
    for copy in loads:
        copy.wait()
    lives = []
    for row in order:
        first = jnp.int32(0)
        for block in range(owner_ref.shape[1]):
            first = first + jnp.where(owner_ref[row, block] == me, block, 0)
        room = len_ref[0, row] - first * slab
        lives.append(lax.broadcasted_iota(jnp.int32, (KVH * QROWS, slab), 1) < room)
    live = stacked(lives)
    places = [(k, row, head) for k, row in enumerate(order) for head in range(KVH)]
    score = stacked(
        [dot_nt(q_ref[row, head], cache_ref[k, :, head_cols(head)]) for k, row, head in places]
    )
    score = jnp.where(live, score * SCALE, NEG)
    top = jnp.max(score, axis=-1, keepdims=True)
    weight = jnp.where(live, jnp.exp(score - top), 0.0)
    total = jnp.sum(weight, axis=-1, keepdims=True)
    safe = jnp.where(total > 0.0, total, 1.0)
    weight = weight.astype(bf16)
    out = stacked(
        [
            dot_nn(
                weight[at * QROWS : (at + 1) * QROWS], cache_ref[k, :, head_cols(head, COLS)]
            )
            for at, (k, _, head) in enumerate(places)
        ]
    )
    out = out / safe
    lse = jnp.where(total > 0.0, top + jnp.log(safe), NEG)
    middle = KVH * QROWS
    put_pair(pair_ref.at[0], 0, out[:middle], lse[:middle])
    put_pair(pair_ref.at[1], 0, out[middle:], lse[middle:])
    for store in stores[2:]:
        store.start()
    for store in stores:
        store.wait()


def absorb_kernel(span_ref, q_hbm, w_hbm, out_hbm, q_ref, w_ref, out_ref, sems):
    part = w_ref.shape[0] // 2
    row = span_ref[0, 0]
    first = pltpu.make_async_copy(q_hbm.at[row], q_ref, sems.at[0])
    parts = [slice(k * part, (k + 1) * part) for k in range(2)]
    loads = [
        pltpu.make_async_copy(w_hbm.at[rows, 0:COLS], w_ref.at[rows], sems.at[1 + k])
        for k, rows in enumerate(parts)
    ]
    stores = [
        pltpu.make_async_copy(out_ref.at[:, cols], out_hbm.at[:, cols], sems.at[3 + k])
        for k, cols in enumerate(parts)
    ]
    for copy in (first, *loads):
        copy.start()
    first.wait()
    for k, cols in enumerate(parts):
        loads[k].wait()
        for head in range(KVH):
            rows = slice(head * QROWS, (head + 1) * QROWS)
            out_ref[rows, cols] = dot_nt(q_ref[head], w_ref[cols, head_cols(head)]).astype(bf16)
        stores[k].start()
    for copy in stores:
        copy.wait()


def other_kernel(qw_ref, acts_ref, out_ref):
    half = acts_ref.shape[0] // 2
    start = pl.multiple_of((1 - lax.axis_index("core")) * half, half)
    score = (dot_nt(qw_ref[...], acts_ref[pl.ds(start, half), :]) * SCALE).astype(bf16)
    for tile in range(half // HD):
        at = tile * QROWS
        out_ref[:, at : at + QROWS] = score[:, head_cols(tile)].reshape(KVH, QROWS, HD)


def own_kernel(qw_ref, acts_ref, own_ref):
    half = acts_ref.shape[0] // 2
    start = pl.multiple_of(lax.axis_index("core") * half, half)
    own_ref[...] = dot_nt(qw_ref[...], acts_ref[pl.ds(start, half), :]) * SCALE


def pack_kernel(got_ref, score_ref, value_ref, own_ref, mine_ref, out_ref):
    half = value_ref.shape[1]
    tiles = half // HD
    out_ref[:, :half] = value_ref[...] + got_ref[:, :half]
    shape = (KVH, QROWS, HD)
    for tile in range(tiles):
        at = tile * QROWS
        score = own_ref[:, head_cols(tile)].reshape(shape)
        score = score + score_ref[:, at : at + QROWS].astype(f32)
        at = half + at
        out_ref[:, at : at + QROWS] = score.astype(bf16)
    at = half + tiles * QROWS
    middle = at + QROWS
    pair = [
        [stat_row(ref[head, first : first + STAT]) for head in range(KVH)]
        for ref, first in ((mine_ref, QROWS), (got_ref, half + QROWS))
    ]
    weights, lse = shares([stacked(rows) for rows in pair])
    weights = columns(stacked(weights))
    packed = [jnp.concatenate(terms(lse[head : head + 1]), axis=0) for head in range(KVH)]
    for head in range(KVH):
        out_ref[head, at:middle] = (
            weights[head] * mine_ref[head, :QROWS].astype(f32)
            + weights[KVH + head] * got_ref[head, half : half + QROWS].astype(f32)
        ).astype(bf16)
        out_ref[head, middle : middle + STAT] = jnp.concatenate(
            [packed[head], jnp.zeros((STAT - 3, HD), f32)], axis=0
        ).astype(bf16)


def span_kernel(got_ref, q_ref, draft_ref, out_ref):
    parts, length, _ = got_ref.shape
    half = (length - PAIR) * HD // (HD + QROWS)
    tiles = half // HD
    role = lax.axis_index("role")
    core = lax.axis_index("core")
    head = lax.axis_index("yx")

    def total(start, size):
        acc = got_ref[0, start : start + size].astype(f32)
        for part in range(1, parts):
            acc = acc + got_ref[part, start : start + size].astype(f32)
        return acc

    value = total(0, half).astype(bf16)
    score = jnp.concatenate(
        [total(half + tile * QROWS, QROWS) for tile in range(tiles)], axis=1
    )
    out, lse = attend(score, value)
    fresh = stacked([out.astype(bf16), packed_stat(lse)])

    query = q_ref[core, head]
    start = pl.multiple_of(head * HD, HD)
    draft_keys = draft_ref[core, :, pl.ds(start, HD)].astype(f32)
    draft_vals = draft_ref[core, :, pl.ds(start + COLS, HD)].astype(f32)
    token = lax.broadcasted_iota(jnp.int32, (QROWS, 1), 0) % DRAFT
    scores = []
    for u in range(DRAFT):
        one = jnp.sum(query.astype(f32) * draft_keys[u : u + 1], axis=-1, keepdims=True) * SCALE
        scores.append(jnp.where(token >= u, one, NEG))
    top = functools.reduce(jnp.maximum, scores)
    weights = [jnp.where(one > 0.5 * NEG, jnp.exp(one - top), 0.0) for one in scores]
    sums = functools.reduce(jnp.add, weights)
    drafted = functools.reduce(
        jnp.add,
        [w.astype(bf16).astype(f32) * draft_vals[u : u + 1] for u, w in enumerate(weights)],
    )
    at = half + tiles * QROWS
    middle = at + QROWS
    rows = [stat_row(got_ref[part, middle : middle + STAT]) for part in range(parts)]
    rows.append(stat_row(packed_stat(top + jnp.log(sums))))
    weights, lse = shares(rows)
    weights = columns(stacked(weights))
    out = weights[parts] * (drafted / sums)
    for part in range(parts):
        out = out + weights[part] * got_ref[part, at:middle].astype(f32)
    spare = jnp.zeros((STAT - 3, HD), f32)
    kept = stacked([out.astype(bf16), stacked([*terms(lse), spare]).astype(bf16)])

    chunks = out_ref.shape[1]
    for chunk in range(chunks):
        out_ref[role, chunk] = kept
        out_ref[1 - role, chunk] = fresh


def join_kernel(span_ref, got_ref, out_hbm, out_ref, sems):
    role = lax.axis_index("role")
    rows = out_ref.shape[0]
    stores = [
        pltpu.make_async_copy(out_ref.at[row], out_hbm.at[row], sems.at[row])
        for row in range(rows)
    ]

    def stats(pool, core):
        return stacked([stat_row(got_ref[pool, 2 * head + core, QROWS:]) for head in range(KVH)])

    fresh = [stats(1 - role, core) for core in range(2)]
    weights = []
    for row in range(rows):
        taken = span_ref[0, 0] == row
        kept = [jnp.where(taken, lse, NEG) for lse in fresh]
        weights += shares([stats(role, row), *kept])[0]
    weights = columns(stacked(weights))
    for row in range(rows):
        for head in range(KVH):
            sources = [(role, row), (1 - role, 0), (1 - role, 1)]
            out = jnp.zeros((QROWS, HD), f32)
            for k, (pool, core) in enumerate(sources):
                weight = weights[(row * 3 + k) * KVH + head]
                out = out + weight * got_ref[pool, 2 * head + core, :QROWS].astype(f32)
            out_ref[row, head] = out.astype(bf16)
        stores[row].start()
    for store in stores:
        store.wait()


def call(kernel, out_shapes, spaces, scratch=(), flops=0, moved=0, limit=24, out_space=pltpu.VMEM):
    out_specs = jax.tree.map(lambda _: pl.BlockSpec(memory_space=out_space), out_shapes)
    return pl.pallas_call(
        kernel,
        out_shape=out_shapes,
        in_specs=[pl.BlockSpec(memory_space=space) for space in spaces],
        out_specs=out_specs,
        scratch_shapes=list(scratch),
        compiler_params=pltpu.CompilerParams(vmem_limit_bytes=limit << 20),
        cost_estimate=pl.CostEstimate(flops=flops, bytes_accessed=moved, transcendentals=0),
    )


V = pltpu.VMEM
S = pltpu.SMEM
H = pltpu.HBM
FRONT = 58


def shards(
    prompt_acts, kv_weight, cache_kv, cache_len, block_owner, span_row, draft_query, draft_kv
):
    swap = [(0, 1), (1, 0)]
    acts = prompt_acts[0, 0]
    span, width = acts.shape
    half = span // 2
    rows = cache_kv.shape[1]
    n_yx = lax.axis_size("yx")
    struct = jax.ShapeDtypeStruct

    query = draft_query[0].reshape(rows, DRAFT, KVH, GROUP, HD).transpose(0, 2, 3, 1, 4)
    query = query.reshape(rows, KVH, QROWS, HD)
    dma = pltpu.SemaphoreType.DMA
    absorbed = call(
        absorb_kernel,
        struct((KVH * QROWS, width), bf16),
        [S, H, H],
        [
            V(query.shape[1:], bf16),
            V((width, COLS), bf16),
            V((KVH * QROWS, width), bf16),
            dma((5,)),
        ],
        flops=70_000_000,
        moved=1_500_000,
        limit=FRONT,
        out_space=H,
    )(span_row, query, kv_weight)
    asked = lax.ppermute(absorbed, "role", swap)
    absorbed, own_query = lax.optimization_barrier((absorbed, query))

    words = (half // HD) * QROWS
    away = struct((KVH, half + PAIR, HD), bf16)
    away, value, mine = call(
        front_kernel,
        [away, struct((KVH, half, HD), bf16), struct((KVH, PAIR, HD), bf16)],
        [H] * 6,
        [
            S(block_owner.shape[1:], jnp.int32),
            S(cache_len.shape, jnp.int32),
            V(query.shape, bf16),
            V(cache_kv.shape[1:], bf16),
            V((2, half, width), bf16),
            V((width, COLS), bf16),
            V((2, KVH, half, HD), bf16),
            V((2, KVH, PAIR, HD), bf16),
            dma((12,)),
        ],
        flops=1_500_000_000,
        moved=6_000_000,
        limit=FRONT,
        out_space=H,
    )(block_owner[0], cache_len, own_query, cache_kv[0], acts, kv_weight)
    theirs = lax.ppermute(away, "core", swap)
    asked, value = lax.optimization_barrier((asked, value))
    score = call(
        other_kernel,
        struct((KVH, words, HD), bf16),
        [V, V],
        flops=140_000_000,
        moved=1_000_000,
    )(asked, acts)
    score = lax.ppermute(score, "core", swap)
    own = call(
        own_kernel,
        struct((KVH * QROWS, half), f32),
        [V, V],
        flops=10_000_000_000,
        moved=2_000_000,
    )(asked, acts)
    sent = call(
        pack_kernel,
        struct((KVH, half + (half // HD) * QROWS + PAIR, HD), bf16),
        [V] * 5,
        flops=10_000_000,
        moved=5_000_000,
    )(theirs, score, value, own, mine)
    got = lax.all_to_all(sent, "yx", 0, 0, tiled=True)

    parts = call(
        span_kernel,
        struct((2, 2 * n_yx, PAIR, HD), bf16),
        [V, V, V],
        flops=20_000_000,
        moved=3_000_000,
    )(got, query, draft_kv[0])
    parts = lax.all_to_all(
        parts.reshape(4 * n_yx, PAIR, HD), ("role", "yx", "core"), 0, 0, tiled=True
    )
    joined = struct((rows, KVH, QROWS, HD), bf16)
    joined = call(
        join_kernel,
        joined,
        [S, V],
        [V(joined.shape, bf16), dma((rows,))],
        flops=10_000_000,
        moved=700_000,
        out_space=H,
    )(span_row, parts.reshape(2, 2 * n_yx, PAIR, HD))
    output = joined.reshape(rows, KVH, GROUP, DRAFT, HD).transpose(0, 3, 1, 2, 4)
    return output.reshape(1, rows, DRAFT, QH * HD)


def solution(mesh):
    roles, groups, tps = mesh.devices.shape
    fine = Mesh(mesh.devices.reshape(roles, groups, tps // 2, 2), ("role", "grp", "yx", "core"))
    tp = ("yx", "core")
    placed = (
        P("role", "grp", None, tp),
        P(tp, None),
        P("role", "grp", tp, None),
        P("role", "grp"),
        P("role", "grp", None),
        P("role", "grp"),
        P("role", "grp", None, None),
        P("role", "grp", None, None),
    )
    return jax.shard_map(
        shards, mesh=fine, in_specs=placed, out_specs=P("role", "grp", None, None), check_vma=False
    )
```

```python
import functools
import math

import jax
import jax.numpy as jnp
from jax import lax
from jax.experimental import pallas as pl
from jax.experimental.pallas import tpu as pltpu
from jax.sharding import Mesh
from jax.sharding import PartitionSpec as P

QH = 64
KVH = 8
HD = 128
DRAFT = 4
GROUP = QH // KVH
QROWS = GROUP * DRAFT
STAT = 16
PAIR = QROWS + STAT
COLS = KVH * HD
NEG = -1e30
SCALE = 1.0 / math.sqrt(HD)

f32 = jnp.float32
bf16 = jnp.bfloat16


def dot_nt(a, b):
    return lax.dot_general(a, b, (((1,), (1,)), ((), ())), preferred_element_type=f32)


def dot_nn(a, b):
    return jnp.dot(a, b, preferred_element_type=f32)


def terms(lse):
    hi = lse.astype(bf16).astype(f32)
    mid = (lse - hi).astype(bf16).astype(f32)
    return hi, mid, lse - hi - mid


def packed_stat(lse):
    lane = lax.broadcasted_iota(jnp.int32, (QROWS, HD), 1)
    tile = jnp.zeros((QROWS, HD), f32)
    for at, term in enumerate(terms(lse)):
        tile = jnp.where(lane == at, term, tile)
    rows = tile.T[:STAT]
    return jnp.concatenate([rows, jnp.zeros((STAT, HD - QROWS), f32)], axis=1).astype(bf16)


def packed_stats(lse):
    count = lse.shape[0] // QROWS
    lane = lax.broadcasted_iota(jnp.int32, (QROWS, HD), 1)
    tile = jnp.zeros((QROWS, HD), f32)
    for head in range(count):
        tile = jnp.where(lane >> 3 == head, lse[head * QROWS : (head + 1) * QROWS], tile)
    term = lane & 7
    packed = jnp.zeros((QROWS, HD), f32)
    for at, part in enumerate(terms(tile)):
        packed = jnp.where(term == at, part, packed)
    rows = jnp.concatenate([packed.T, jnp.zeros((HD, HD - QROWS), f32)], axis=1)
    spare = jnp.zeros((STAT - 8, HD), f32)
    return [
        jnp.concatenate([rows[head * 8 : head * 8 + 8], spare], axis=0).astype(bf16)
        for head in range(count)
    ]


def stat_row(tile):
    rows = tile.astype(f32)
    return rows[0:1] + rows[1:2] + rows[2:3]


def columns(rows):
    count = rows.shape[0]
    square = jnp.concatenate([rows, jnp.zeros((HD - count, HD), f32)], axis=0).T
    return [square[:QROWS, k : k + 1] for k in range(count)]


def attend(score, value):
    top = jnp.max(score, axis=-1, keepdims=True)
    weight = jnp.where(score > 0.5 * NEG, jnp.exp(score - top), 0.0)
    total = jnp.sum(weight, axis=-1, keepdims=True)
    any_key = total > 0.0
    safe = jnp.where(any_key, total, 1.0)
    out = dot_nn(weight.astype(bf16), value) / safe
    return out, jnp.where(any_key, top + jnp.log(safe), NEG)


def shares(rows):
    top = functools.reduce(jnp.maximum, rows)
    weights = [jnp.where(row > 0.5 * NEG, jnp.exp(row - top), 0.0) for row in rows]
    total = functools.reduce(jnp.add, weights)
    safe = jnp.where(total > 0.0, total, 1.0)
    return [w / safe for w in weights], jnp.where(total > 0.0, top + jnp.log(safe), NEG)


def stacked(parts):
    return jnp.concatenate(parts, axis=0)


def head_cols(head, start=0):
    return slice(start + head * HD, start + (head + 1) * HD)


def front_kernel(
    owner_hbm,
    len_hbm,
    q_hbm,
    cache_hbm,
    acts_hbm,
    w_hbm,
    away_hbm,
    value_hbm,
    mine_hbm,
    owner_ref,
    len_ref,
    q_ref,
    cache_ref,
    acts_ref,
    w_ref,
    value_ref,
    pair_ref,
    sems,
):
    core = lax.axis_index("core")
    me = lax.axis_index("yx") * 2 + core
    slab = cache_ref.shape[1]
    half = acts_ref.shape[1]
    order = (1 - core, core)
    early = [pltpu.make_async_copy(w_hbm.at[:, COLS : 2 * COLS], w_ref, sems.at[6])]
    early += [
        pltpu.make_async_copy(
            acts_hbm.at[pl.ds(pl.multiple_of(row * half, half), half)], acts_ref.at[k], sems.at[at]
        )
        for k, (row, at) in enumerate(zip(order, (5, 11)))
    ]
    loads = [
        pltpu.make_async_copy(owner_hbm, owner_ref, sems.at[0]),
        pltpu.make_async_copy(len_hbm, len_ref, sems.at[1]),
        pltpu.make_async_copy(q_hbm, q_ref, sems.at[2]),
    ]
    loads += [
        pltpu.make_async_copy(cache_hbm.at[row], cache_ref.at[k], sems.at[3 + k])
        for k, row in enumerate(order)
    ]
    stores = [
        pltpu.make_async_copy(value_ref.at[0], away_hbm.at[:, :half], sems.at[7]),
        pltpu.make_async_copy(value_ref.at[1], value_hbm, sems.at[8]),
        pltpu.make_async_copy(pair_ref.at[0], away_hbm.at[:, half : half + PAIR], sems.at[9]),
        pltpu.make_async_copy(pair_ref.at[1], mine_hbm, sems.at[10]),
    ]
    for copy in (*early, *loads):
        copy.start()
    early[0].wait()
    for k in range(2):
        early[1 + k].wait()
        value = dot_nn(acts_ref[k], w_ref[...]).astype(bf16)
        for head in range(KVH):
            value_ref[k, head] = value[:, head_cols(head)]
        stores[k].start()
    for copy in loads:
        copy.wait()
    lives = []
    for row in order:
        first = jnp.int32(0)
        for block in range(owner_ref.shape[1]):
            first = first + jnp.where(owner_ref[row, block] == me, block, 0)
        room = len_ref[0, row] - first * slab
        lives.append(lax.broadcasted_iota(jnp.int32, (KVH * QROWS, slab), 1) < room)
    live = stacked(lives)
    places = [(k, row, head) for k, row in enumerate(order) for head in range(KVH)]
    score = stacked(
        [dot_nt(q_ref[row, head], cache_ref[k, :, head_cols(head)]) for k, row, head in places]
    )
    score = jnp.where(live, score * SCALE, NEG)
    top = jnp.max(score, axis=-1, keepdims=True)
    weight = jnp.where(live, jnp.exp(score - top), 0.0)
    total = jnp.sum(weight, axis=-1, keepdims=True)
    safe = jnp.where(total > 0.0, total, 1.0)
    weight = weight.astype(bf16)
    out = stacked(
        [
            dot_nn(
                weight[at * QROWS : (at + 1) * QROWS], cache_ref[k, :, head_cols(head, COLS)]
            )
            for at, (k, _, head) in enumerate(places)
        ]
    )
    out = out / safe
    lse = jnp.where(total > 0.0, top + jnp.log(safe), NEG)
    packed = packed_stats(lse)
    for at, (k, _, head) in enumerate(places):
        pair_ref[k, head, :QROWS] = out[at * QROWS : (at + 1) * QROWS].astype(bf16)
        pair_ref[k, head, QROWS:] = packed[at]
    for store in stores[2:]:
        store.start()
    for store in stores:
        store.wait()


def absorb_kernel(span_ref, q_hbm, w_hbm, out_hbm, q_ref, w_ref, out_ref, sems):
    part = w_ref.shape[0] // 2
    row = span_ref[0, 0]
    first = pltpu.make_async_copy(q_hbm.at[row], q_ref, sems.at[0])
    parts = [slice(k * part, (k + 1) * part) for k in range(2)]
    loads = [
        pltpu.make_async_copy(w_hbm.at[rows, 0:COLS], w_ref.at[rows], sems.at[1 + k])
        for k, rows in enumerate(parts)
    ]
    stores = [
        pltpu.make_async_copy(out_ref.at[:, cols], out_hbm.at[:, cols], sems.at[3 + k])
        for k, cols in enumerate(parts)
    ]
    for copy in (first, *loads):
        copy.start()
    first.wait()
    for k, cols in enumerate(parts):
        loads[k].wait()
        for head in range(KVH):
            rows = slice(head * QROWS, (head + 1) * QROWS)
            out_ref[rows, cols] = dot_nt(q_ref[head], w_ref[cols, head_cols(head)]).astype(bf16)
        stores[k].start()
    for copy in stores:
        copy.wait()


def other_kernel(qw_ref, acts_ref, out_ref):
    half = acts_ref.shape[0] // 2
    start = pl.multiple_of((1 - lax.axis_index("core")) * half, half)
    score = (dot_nt(qw_ref[...], acts_ref[pl.ds(start, half), :]) * SCALE).astype(bf16)
    for tile in range(half // HD):
        at = tile * QROWS
        out_ref[:, at : at + QROWS] = score[:, head_cols(tile)].reshape(KVH, QROWS, HD)


def own_kernel(qw_ref, acts_ref, own_ref):
    half = acts_ref.shape[0] // 2
    start = pl.multiple_of(lax.axis_index("core") * half, half)
    own_ref[...] = dot_nt(qw_ref[...], acts_ref[pl.ds(start, half), :]) * SCALE


def pack_kernel(got_ref, score_ref, value_ref, own_ref, mine_ref, out_ref):
    half = value_ref.shape[1]
    tiles = half // HD
    out_ref[:, :half] = value_ref[...] + got_ref[:, :half]
    shape = (KVH, QROWS, HD)
    for tile in range(tiles):
        at = tile * QROWS
        score = own_ref[:, head_cols(tile)].reshape(shape)
        score = score + score_ref[:, at : at + QROWS].astype(f32)
        at = half + at
        out_ref[:, at : at + QROWS] = score.astype(bf16)
    at = half + tiles * QROWS
    middle = at + QROWS
    pair = [
        [stat_row(ref[head, first : first + STAT]) for head in range(KVH)]
        for ref, first in ((mine_ref, QROWS), (got_ref, half + QROWS))
    ]
    weights, lse = shares([stacked(rows) for rows in pair])
    weights = columns(stacked(weights))
    packed = [jnp.concatenate(terms(lse[head : head + 1]), axis=0) for head in range(KVH)]
    for head in range(KVH):
        out_ref[head, at:middle] = (
            weights[head] * mine_ref[head, :QROWS].astype(f32)
            + weights[KVH + head] * got_ref[head, half : half + QROWS].astype(f32)
        ).astype(bf16)
        out_ref[head, middle : middle + STAT] = jnp.concatenate(
            [packed[head], jnp.zeros((STAT - 3, HD), f32)], axis=0
        ).astype(bf16)


def span_kernel(got_ref, q_ref, draft_ref, out_ref):
    parts, length, _ = got_ref.shape
    half = (length - PAIR) * HD // (HD + QROWS)
    tiles = half // HD
    role = lax.axis_index("role")
    core = lax.axis_index("core")
    head = lax.axis_index("yx")

    def total(start, size):
        acc = got_ref[0, start : start + size].astype(f32)
        for part in range(1, parts):
            acc = acc + got_ref[part, start : start + size].astype(f32)
        return acc

    value = total(0, half).astype(bf16)
    score = jnp.concatenate(
        [total(half + tile * QROWS, QROWS) for tile in range(tiles)], axis=1
    )
    out, lse = attend(score, value)
    fresh = stacked([out.astype(bf16), packed_stat(lse)])

    query = q_ref[core, head]
    start = pl.multiple_of(head * HD, HD)
    draft_keys = draft_ref[core, :, pl.ds(start, HD)].astype(f32)
    draft_vals = draft_ref[core, :, pl.ds(start + COLS, HD)].astype(f32)
    token = lax.broadcasted_iota(jnp.int32, (QROWS, 1), 0) % DRAFT
    scores = []
    for u in range(DRAFT):
        one = jnp.sum(query.astype(f32) * draft_keys[u : u + 1], axis=-1, keepdims=True) * SCALE
        scores.append(jnp.where(token >= u, one, NEG))
    top = functools.reduce(jnp.maximum, scores)
    weights = [jnp.where(one > 0.5 * NEG, jnp.exp(one - top), 0.0) for one in scores]
    sums = functools.reduce(jnp.add, weights)
    drafted = functools.reduce(
        jnp.add,
        [w.astype(bf16).astype(f32) * draft_vals[u : u + 1] for u, w in enumerate(weights)],
    )
    at = half + tiles * QROWS
    middle = at + QROWS
    rows = [stat_row(got_ref[part, middle : middle + STAT]) for part in range(parts)]
    rows.append(stat_row(packed_stat(top + jnp.log(sums))))
    weights, lse = shares(rows)
    weights = columns(stacked(weights))
    out = weights[parts] * (drafted / sums)
    for part in range(parts):
        out = out + weights[part] * got_ref[part, at:middle].astype(f32)
    spare = jnp.zeros((STAT - 3, HD), f32)
    kept = stacked([out.astype(bf16), stacked([*terms(lse), spare]).astype(bf16)])

    chunks = out_ref.shape[1]
    for chunk in range(chunks):
        out_ref[role, chunk] = kept
        out_ref[1 - role, chunk] = fresh


def join_kernel(span_ref, got_ref, out_hbm, out_ref, sems):
    role = lax.axis_index("role")
    rows = out_ref.shape[0]
    stores = [
        pltpu.make_async_copy(out_ref.at[row], out_hbm.at[row], sems.at[row])
        for row in range(rows)
    ]

    def stats(pool, core):
        return stacked([stat_row(got_ref[pool, 2 * head + core, QROWS:]) for head in range(KVH)])

    fresh = [stats(1 - role, core) for core in range(2)]
    weights = []
    for row in range(rows):
        taken = span_ref[0, 0] == row
        kept = [jnp.where(taken, lse, NEG) for lse in fresh]
        weights += shares([stats(role, row), *kept])[0]
    weights = columns(stacked(weights))
    for row in range(rows):
        for head in range(KVH):
            sources = [(role, row), (1 - role, 0), (1 - role, 1)]
            out = jnp.zeros((QROWS, HD), f32)
            for k, (pool, core) in enumerate(sources):
                weight = weights[(row * 3 + k) * KVH + head]
                out = out + weight * got_ref[pool, 2 * head + core, :QROWS].astype(f32)
            out_ref[row, head] = out.astype(bf16)
        stores[row].start()
    for store in stores:
        store.wait()


def call(kernel, out_shapes, spaces, scratch=(), flops=0, moved=0, limit=24, out_space=pltpu.VMEM):
    out_specs = jax.tree.map(lambda _: pl.BlockSpec(memory_space=out_space), out_shapes)
    return pl.pallas_call(
        kernel,
        out_shape=out_shapes,
        in_specs=[pl.BlockSpec(memory_space=space) for space in spaces],
        out_specs=out_specs,
        scratch_shapes=list(scratch),
        compiler_params=pltpu.CompilerParams(vmem_limit_bytes=limit << 20),
        cost_estimate=pl.CostEstimate(flops=flops, bytes_accessed=moved, transcendentals=0),
    )


V = pltpu.VMEM
S = pltpu.SMEM
H = pltpu.HBM
FRONT = 58


def shards(
    prompt_acts, kv_weight, cache_kv, cache_len, block_owner, span_row, draft_query, draft_kv
):
    swap = [(0, 1), (1, 0)]
    acts = prompt_acts[0, 0]
    span, width = acts.shape
    half = span // 2
    rows = cache_kv.shape[1]
    n_yx = lax.axis_size("yx")
    struct = jax.ShapeDtypeStruct

    query = draft_query[0].reshape(rows, DRAFT, KVH, GROUP, HD).transpose(0, 2, 3, 1, 4)
    query = query.reshape(rows, KVH, QROWS, HD)
    dma = pltpu.SemaphoreType.DMA
    absorbed = call(
        absorb_kernel,
        struct((KVH * QROWS, width), bf16),
        [S, H, H],
        [
            V(query.shape[1:], bf16),
            V((width, COLS), bf16),
            V((KVH * QROWS, width), bf16),
            dma((5,)),
        ],
        flops=70_000_000,
        moved=1_500_000,
        limit=FRONT,
        out_space=H,
    )(span_row, query, kv_weight)
    asked = lax.ppermute(absorbed, "role", swap)
    absorbed, own_query = lax.optimization_barrier((absorbed, query))

    words = (half // HD) * QROWS
    away = struct((KVH, half + PAIR, HD), bf16)
    away, value, mine = call(
        front_kernel,
        [away, struct((KVH, half, HD), bf16), struct((KVH, PAIR, HD), bf16)],
        [H] * 6,
        [
            S(block_owner.shape[1:], jnp.int32),
            S(cache_len.shape, jnp.int32),
            V(query.shape, bf16),
            V(cache_kv.shape[1:], bf16),
            V((2, half, width), bf16),
            V((width, COLS), bf16),
            V((2, KVH, half, HD), bf16),
            V((2, KVH, PAIR, HD), bf16),
            dma((12,)),
        ],
        flops=1_500_000_000,
        moved=6_000_000,
        limit=FRONT,
        out_space=H,
    )(block_owner[0], cache_len, own_query, cache_kv[0], acts, kv_weight)
    theirs = lax.ppermute(away, "core", swap)
    asked, value = lax.optimization_barrier((asked, value))
    score = call(
        other_kernel,
        struct((KVH, words, HD), bf16),
        [V, V],
        flops=140_000_000,
        moved=1_000_000,
    )(asked, acts)
    score = lax.ppermute(score, "core", swap)
    own = call(
        own_kernel,
        struct((KVH * QROWS, half), f32),
        [V, V],
        flops=10_000_000_000,
        moved=2_000_000,
    )(asked, acts)
    sent = call(
        pack_kernel,
        struct((KVH, half + (half // HD) * QROWS + PAIR, HD), bf16),
        [V] * 5,
        flops=10_000_000,
        moved=5_000_000,
    )(theirs, score, value, own, mine)
    got = lax.all_to_all(sent, "yx", 0, 0, tiled=True)

    parts = call(
        span_kernel,
        struct((2, 2 * n_yx, PAIR, HD), bf16),
        [V, V, V],
        flops=20_000_000,
        moved=3_000_000,
    )(got, query, draft_kv[0])
    parts = lax.all_to_all(
        parts.reshape(4 * n_yx, PAIR, HD), ("role", "yx", "core"), 0, 0, tiled=True
    )
    joined = struct((rows, KVH, QROWS, HD), bf16)
    joined = call(
        join_kernel,
        joined,
        [S, V],
        [V(joined.shape, bf16), dma((rows,))],
        flops=10_000_000,
        moved=700_000,
        out_space=H,
    )(span_row, parts.reshape(2, 2 * n_yx, PAIR, HD))
    output = joined.reshape(rows, KVH, GROUP, DRAFT, HD).transpose(0, 3, 1, 2, 4)
    return output.reshape(1, rows, DRAFT, QH * HD)


def solution(mesh):
    roles, groups, tps = mesh.devices.shape
    fine = Mesh(mesh.devices.reshape(roles, groups, tps // 2, 2), ("role", "grp", "yx", "core"))
    tp = ("yx", "core")
    placed = (
        P("role", "grp", None, tp),
        P(tp, None),
        P("role", "grp", tp, None),
        P("role", "grp"),
        P("role", "grp", None),
        P("role", "grp"),
        P("role", "grp", None, None),
        P("role", "grp", None, None),
    )
    return jax.shard_map(
        shards, mesh=fine, in_specs=placed, out_specs=P("role", "grp", None, None), check_vma=False
    )
```
